256 devices in a mesh: ctx: 32 (over x_hi, z, core), head: 8 (over x_lo, y).
Axes of the slice: x: 4 (x_hi: 2, x_lo: 2; x = x_hi * 2 + x_lo), y: 4, z: 8, core: 2. Of those that a mesh axis runs over, the one named last changes fastest.
Arguments:
- queries: bfloat16 [4096, 2048], P('ctx', 'head'), may hold values from -6 to 6
- key_rows: bfloat16 [4096, 2048], P('ctx', 'head'), may hold values from -6 to 6
- value_rows: bfloat16 [4096, 2048], P('ctx', 'head'), may hold values from -13 to 13
- output_weight: bfloat16 [2048, 2048], P('head'), may hold values from -1 to 1
- residual_stream: bfloat16 [4096, 2048], P('ctx', 'head'), may hold values from -0.3125 to 0.3125
- norm_gain: float32 [2048], P('head'), may hold values from 0.1 to 1.9
- expert_ids: int32 [4096, 6], P('ctx'), may hold values from 0 to 63, all different within a row; in each aligned block of 128 rows (0 to 127, 128 to 255, ...) at most 16 rows name the same one
- combine_weights: float32 [4096, 6], P('ctx'), may hold values from 0.2 to 1
- gate_weight: bfloat16 [64, 1408, 2048], P('ctx', 'head'), may hold values from -0.125 to 0.125
- up_weight: bfloat16 [64, 1408, 2048], P('ctx', 'head'), may hold values from -0.125 to 0.125
- down_weight: bfloat16 [64, 1408, 2048], P('ctx', 'head'), may hold values from -0.15625 to 0.15625
- cotangent: bfloat16 [4096, 2048], P('ctx', 'head'), may hold values from -13 to 13
Outputs:
- moe_output: bfloat16 [4096, 2048], P('ctx', 'head')
- attention_grad: bfloat16 [4096, 2048], P('ctx', 'head')
- residual_grad: bfloat16 [4096, 2048], P('ctx', 'head')
- gain_grad: float32 [2048], P('head')
- combine_grad: float32 [4096, 6], P('ctx')
- gate_grad: bfloat16 [64, 1408, 2048], P('ctx', 'head')
- up_grad: bfloat16 [64, 1408, 2048], P('ctx', 'head')
- down_grad: bfloat16 [64, 1408, 2048], P('ctx', 'head')
The draws below stay inside these ranges and needn't reach their ends.
Inputs may be any that keep to these rules, and one draw needn't show every extreme that they name: `expert_ids`: each row names 6 different experts. In every aligned block of 128 rows (the rows of one device) no expert is named more than 16 times, and in some blocks one expert is named exactly 16 times.
All inputs are finite; a program needn't handle non-finite values.
Results may differ from the reference program's by a relative error of at most 0.035.
Values may be sent and summed in bfloat16 or wider, within the bound.
A program may use at most 128 MiB of HBM per device.

```python
import math
import jax
import jax.numpy as jnp
import numpy as np
from jax import lax

D = 2048
HEADS = 16
F = 1408
TOP = 6
TOK_DEV = 128
E = 64
DH = 128
TOKENS = 4096
CAP = 16
N_CTX = 32
N_HEAD = 8


def column_rise(exponent):
    column_ids = jnp.arange(D, dtype=jnp.float32)
    return jnp.power(10.0, exponent * (column_ids / D - 0.5))


def draw_queries(key, part):
    key = jax.random.fold_in(key, 11)
    drawn = jax.random.truncated_normal(key, -4.0, 4.0, (TOKENS, D), jnp.float32)
    return drawn.astype(jnp.bfloat16)


def draw_key_rows(key, part):
    key = jax.random.fold_in(key, 12)
    drawn = jax.random.truncated_normal(key, -4.0, 4.0, (TOKENS, D), jnp.float32)
    return drawn.astype(jnp.bfloat16)


def draw_value_rows(key, part):
    key = jax.random.fold_in(key, 13)
    first_key = jax.random.fold_in(key, 0)
    column_ids = jnp.arange(D, dtype=jnp.float32)
    column_scale = jnp.power(10.0, column_ids / D - 0.5)
    drawn = jax.random.truncated_normal(first_key, -4.0, 4.0, (TOKENS, D), jnp.float32)
    return (drawn * column_scale[None, :]).astype(jnp.bfloat16)


def draw_output_weight(key, part):
    key = jax.random.fold_in(key, 15)
    drawn = jax.random.truncated_normal(key, -4.0, 4.0, (D, D), jnp.float32) * column_rise(0.35)[None, :]
    return (drawn * D ** (-0.5)).astype(jnp.bfloat16)


def draw_cotangent(key, part):
    key = jax.random.fold_in(key, 14)
    row_ids = jnp.arange(TOKENS, dtype=jnp.float32)
    column_ids = jnp.arange(D, dtype=jnp.float32)
    both_scale = jnp.power(10.0, 0.5 * (row_ids[:, None] / TOKENS + column_ids[None, :] / D) - 0.5)
    drawn = jax.random.truncated_normal(key, -4.0, 4.0, (TOKENS, D), jnp.float32)
    return (drawn * both_scale).astype(jnp.bfloat16)


def block_levels(rng, extent, pieces, smallest, largest):
    level = 1.0
    for axis_at, blocks in pieces:
        heights = jax.random.uniform(jax.random.fold_in(jax.random.fold_in(rng, 6), axis_at), (blocks,), jnp.float32, smallest / len(pieces), largest / len(pieces))
        level = level * jnp.repeat(jnp.exp(heights), extent[axis_at] // blocks).reshape((-1,) + (1,) * (len(extent) - 1 - axis_at))
    return level


def deal_out(own_key, own, number, rows, amount, top, limit, lean):
    order = jax.random.permutation(own_key, amount)
    heavy_load, ordinary = portions_of(amount, rows * top, limit, lean, True), portions_of(amount, rows * top, limit, lean, False)
    places = jnp.arange(amount)

    def named(tallies, offset_by):
        used = int((tallies > 0).sum())
        fixed = max(1, used // 4)
        passed = fixed + (places - fixed + offset_by * (used - fixed)) % max(1, amount - fixed)
        return jnp.zeros((amount,), jnp.int32).at[order[jnp.where(places < fixed, places, passed)]].set(jnp.asarray(tallies, jnp.int32))

    tallies = jnp.where(number % 4 == 0, named(heavy_load, number // 4), named(ordinary, number - number // 4 - 1))
    mixed = jax.random.permutation(jax.random.fold_in(own, 3), amount)
    giver, taker = mixed[0:amount // 2 * 2:2], mixed[1:amount // 2 * 2:2]
    slack = jnp.minimum(tallies[giver] - 1, limit - tallies[taker]) // 2
    slack = jnp.where((giver == order[0]) | (taker == order[0]) | (tallies[taker] == 0), 0, jnp.maximum(slack, 0))
    passed = jax.random.randint(jax.random.fold_in(own, 4), (amount // 2,), 0, 1 << 20) % (slack + 1)
    tallies = tallies.at[giver].add(-passed).at[taker].add(passed)
    members = jnp.searchsorted(jnp.cumsum(tallies), jnp.arange(rows * top), side="right").astype(jnp.int32)
    grid = members.reshape(top, rows).T
    grid = grid[jax.random.permutation(jax.random.fold_in(own, 1), rows)]
    offset_by = jax.random.randint(jax.random.fold_in(own, 2), (rows, 1), 0, top)
    return jnp.take_along_axis(grid, (jnp.arange(top)[None, :] + offset_by) % top, axis=1)


def portions_of(amount, total, most, lean, full):
    portions = [(1 << 20) // math.isqrt(standing ** lean) + 1 for standing in range(1, amount + 1)]
    largest = most if full else min(most, max(-(-total // amount), total * portions[0] // sum(portions)))
    least = 1 if total - largest >= amount - 1 else 0
    given, rest = [largest] + [least] * (amount - 1), total - largest - least * (amount - 1)
    while rest > 0:
        free = [i for i in range(1, amount) if given[i] < largest] or [i for i in range(1, amount) if given[i] < most]
        pool, budget = sum([portions[i] for i in free]), rest
        for i in free:
            more = min(most - given[i], max(1, budget * portions[i] // pool), rest)
            given[i] = given[i] + more
            rest = rest - more
    return np.array(given)


def scatter_about(rng, dims, scale, bound, pieces=(), kind=jnp.bfloat16):
    array = jax.random.normal(rng, dims, jnp.float32) * scale
    if len(pieces) > 0:
        array = block_levels(rng, dims, pieces, -0.22, 0.18) * array
    return jnp.clip(array, min=-bound, max=bound).astype(kind)


def setup_inputs(seed: int = 0) -> dict:
    seeds = jax.random.split(jax.random.key(seed), 13)
    queries = draw_queries(jax.random.fold_in(seeds[12], 71), 0)
    key_rows = draw_key_rows(jax.random.fold_in(seeds[12], 71), 0)
    value_rows = draw_value_rows(jax.random.fold_in(seeds[12], 71), 0)
    output_weight = draw_output_weight(jax.random.fold_in(seeds[12], 71), 0)
    residual_stream = scatter_about(seeds[4], (TOKENS, D), 0.02, 0.3125, ((0, 32), (1, 8)))
    norm_gain = jnp.clip(1.0 + 0.18 * jax.random.normal(seeds[5], (D,), jnp.float32), 0.1, 1.9)
    expert_ids_keys = jax.random.split(jax.random.fold_in(seeds[6], 1), TOKENS // TOK_DEV)
    expert_ids_turns = jax.random.permutation(jax.random.fold_in(seeds[6], 3), TOKENS // TOK_DEV)
    expert_ids = jax.vmap(lambda own, number: deal_out(jax.random.fold_in(seeds[6], 2), own, number, TOK_DEV, E, TOP, CAP, 2))(expert_ids_keys, expert_ids_turns).reshape((TOKENS, TOP))
    combine_weights = jnp.clip(0.2 + 0.8 * jax.random.uniform(seeds[7], (TOKENS, TOP), jnp.float32) ** block_levels(seeds[7], (TOKENS, TOP), ((0, 32),), -0.2, 0.2), 0.2, 1.0)
    gate_weight = scatter_about(seeds[8], (E, F, D), D ** -0.5, 0.125, ((0, 32), (1, 8)))
    up_weight = scatter_about(seeds[9], (E, F, D), D ** -0.5, 0.125, ((0, 32), (1, 8)))
    down_weight = scatter_about(seeds[10], (E, F, D), F ** -0.5, 0.15625, ((0, 32), (1, 8)))
    cotangent = draw_cotangent(jax.random.fold_in(seeds[12], 71), 0)
    return dict(queries=queries, key_rows=key_rows, value_rows=value_rows, output_weight=output_weight, residual_stream=residual_stream, norm_gain=norm_gain, expert_ids=expert_ids, combine_weights=combine_weights, gate_weight=gate_weight, up_weight=up_weight, down_weight=down_weight, cotangent=cotangent)


def reference(queries, key_rows, value_rows, output_weight, residual_stream, norm_gain, expert_ids, combine_weights, gate_weight, up_weight, down_weight, cotangent):
    score_scale = DH ** (-0.5)
    query_head_count = queries.reshape(TOKENS, HEADS, DH).transpose(1, 0, 2)
    key_head_count = key_rows.reshape(TOKENS, HEADS, DH).transpose(1, 0, 2)
    value_heads = value_rows.reshape(TOKENS, HEADS, DH).transpose(1, 0, 2)
    positions = jnp.arange(TOKENS, dtype=jnp.int32)
    causal_mask = positions[:, None] >= positions[None, :]

    def one_head(operands):
        query_head, key_head, value_head = operands
        scores = jnp.dot(query_head, key_head.T, preferred_element_type=jnp.float32) * score_scale
        row_max = lax.optimization_barrier(jnp.max(jnp.where(causal_mask, scores, -1e+30), axis=1, keepdims=True))
        weights = jnp.where(causal_mask, jnp.exp(scores - row_max), 0.0)
        totals = lax.optimization_barrier(jnp.sum(weights, axis=1))
        result = jnp.dot(weights.astype(jnp.bfloat16), value_head, preferred_element_type=jnp.float32) / totals[:, None]
        return result.astype(jnp.bfloat16)
    attention = lax.map(one_head, (query_head_count, key_head_count, value_heads)).transpose(1, 0, 2).reshape(TOKENS, D)
    projected = jnp.dot(attention, output_weight, preferred_element_type=jnp.float32)
    hidden_width = residual_stream.astype(jnp.float32) + projected
    inverse = lax.rsqrt(lax.optimization_barrier(jnp.mean(hidden_width * hidden_width, axis=1)) + 1e-06)
    normed = hidden_width * inverse[:, None]
    inputs = (normed * norm_gain).astype(jnp.bfloat16)
    block_ids = expert_ids.reshape(N_CTX, TOK_DEV * TOP)
    onehot = (block_ids[:, :, None] == jnp.arange(E, dtype=jnp.int32)[None, None, :]).astype(jnp.int32)
    earlier = jnp.cumsum(onehot, axis=1) - onehot
    slot_index = lax.optimization_barrier(jnp.sum(earlier * onehot, axis=2)).reshape(TOKENS, TOP)
    source_block = jnp.arange(TOKENS, dtype=jnp.int32) // TOK_DEV
    row_slot = (source_block[:, None] * CAP + slot_index).astype(jnp.int32)
    pick_ids = jnp.arange(TOKENS * TOP, dtype=jnp.int32).reshape(TOKENS, TOP)
    pick_table = jnp.full((E, N_CTX * CAP), TOKENS * TOP, jnp.int32).at[expert_ids, row_slot].set(pick_ids)
    padded_inputs = jnp.concatenate([inputs, jnp.zeros((1, D), jnp.bfloat16)], axis=0)
    padded_cotangent = jnp.concatenate([cotangent, jnp.zeros((1, D), jnp.bfloat16)], axis=0)
    padded_combine = jnp.concatenate([combine_weights.reshape(-1), jnp.zeros((1,), jnp.float32)], axis=0)
    group_width = F // N_HEAD

    def one_expert(operands):
        table_row, gate_weight_part, up_slice, down_slice = operands
        token_of = (table_row // TOP).astype(jnp.int32)
        rows_in = padded_inputs[token_of]
        pick_weight = padded_combine[table_row]
        grad_rows = (pick_weight[:, None] * padded_cotangent[token_of].astype(jnp.float32)).astype(jnp.bfloat16)
        gate_pre = jnp.dot(rows_in, gate_weight_part.T, preferred_element_type=jnp.float32)
        up_pre = jnp.dot(rows_in, up_slice.T, preferred_element_type=jnp.float32)
        sigmoid_gate = jax.nn.sigmoid(gate_pre)
        activation = (gate_pre * sigmoid_gate * up_pre).astype(jnp.bfloat16)
        expert_out = jnp.zeros((N_CTX * CAP, D), jnp.float32)
        for group_index in range(N_HEAD):
            lower = group_index * group_width
            upper = lower + group_width
            term = jnp.dot(activation[:, lower:upper], down_slice[lower:upper], preferred_element_type=jnp.float32)
            rounded = lax.optimization_barrier(term.astype(jnp.bfloat16))
            expert_out = expert_out + rounded.astype(jnp.float32)
        expert_out = expert_out.astype(jnp.bfloat16)
        act_grad = jnp.dot(grad_rows, down_slice.T, preferred_element_type=jnp.float32)
        down_grad = jnp.dot(activation.T, grad_rows, preferred_element_type=jnp.float32).astype(jnp.bfloat16)
        gate_delta = (act_grad * up_pre * sigmoid_gate * (1.0 + gate_pre * (1.0 - sigmoid_gate))).astype(jnp.bfloat16)
        up_delta = (act_grad * gate_pre * sigmoid_gate).astype(jnp.bfloat16)
        gate_grad = jnp.dot(gate_delta.T, rows_in, preferred_element_type=jnp.float32).astype(jnp.bfloat16)
        up_grad = jnp.dot(up_delta.T, rows_in, preferred_element_type=jnp.float32).astype(jnp.bfloat16)
        row_grad = jnp.zeros((N_CTX * CAP, D), jnp.float32)
        for group_index in range(N_HEAD):
            lower = group_index * group_width
            upper = lower + group_width
            term = jnp.dot(gate_delta[:, lower:upper], gate_weight_part[lower:upper], preferred_element_type=jnp.float32)
            term = term + jnp.dot(up_delta[:, lower:upper], up_slice[lower:upper], preferred_element_type=jnp.float32)
            rounded = lax.optimization_barrier(term.astype(jnp.bfloat16))
            row_grad = row_grad + rounded.astype(jnp.float32)
        row_grad = row_grad.astype(jnp.bfloat16)
        return (expert_out, row_grad, gate_grad, up_grad, down_grad)
    expert_out, row_grad, gate_grad, up_grad, down_grad = lax.map(one_expert, (pick_table, gate_weight, up_weight, down_weight))
    picked = expert_out[expert_ids, row_slot]
    moe_output = lax.optimization_barrier(jnp.sum(combine_weights[:, :, None] * picked.astype(jnp.float32), axis=1)).astype(jnp.bfloat16)
    combine_grad = lax.optimization_barrier(jnp.sum(cotangent.astype(jnp.float32)[:, None, :] * picked.astype(jnp.float32), axis=2))
    input_grad = lax.optimization_barrier(jnp.sum(row_grad[expert_ids, row_slot].astype(jnp.float32), axis=1))
    gain_grad = lax.optimization_barrier(jnp.sum(input_grad * normed, axis=0))
    normed_grad = input_grad * norm_gain
    centre = lax.optimization_barrier(jnp.mean(normed_grad * normed, axis=1))
    residual_grad = (inverse[:, None] * (normed_grad - normed * centre[:, None])).astype(jnp.bfloat16)
    attention_grad = jnp.dot(residual_grad, output_weight.T, preferred_element_type=jnp.float32).astype(jnp.bfloat16)
    return (moe_output, attention_grad, residual_grad, gain_grad, combine_grad, gate_grad, up_grad, down_grad)
```

```python
import functools

import jax
import jax.numpy as jnp
from jax import lax
from jax.experimental import pallas as pl
from jax.experimental.pallas import tpu as pltpu
from jax.sharding import PartitionSpec as P

D = 2048
TOP = 6
DH = 128
NC = 32
NH = 8
TOK = 128
W = 256
FD = 176
CAP = 16
ROWS = NC * CAP
SLOTS = 2 * ROWS
MESH = pl.DeviceIdType.MESH
BF = jnp.bfloat16
F32 = jnp.float32


def dot(a, b, ca=1, cb=0):
    return lax.dot_general(a, b, (((ca,), (cb,)), ((), ())), preferred_element_type=F32)


def coords():
    return lax.axis_index("ctx"), lax.axis_index("head")


def head_of(xl, y):
    return xl * 4 + lax.rem(y + 4, 4)


def ctx_of(xh, z, core):
    return xh * 16 + lax.rem(z + 8, 8) * 2 + core


def remote(src, dst, ssem, rsem, ctx, head):
    return pltpu.make_async_remote_copy(
        src, dst, ssem, rsem, device_id=(ctx, head), device_id_type=MESH
    )


def greet():
    i, h = coords()
    bar = pltpu.get_barrier_semaphore()

    def ctx_peer(o, c):
        pl.semaphore_signal(bar, 1, device_id=(lax.rem(i + o, NC), h), device_id_type=MESH)
        return c

    def head_peer(o, c):
        pl.semaphore_signal(bar, 1, device_id=(i, lax.rem(h + o, NH)), device_id_type=MESH)
        return c

    lax.fori_loop(1, NC, ctx_peer, 0)
    lax.fori_loop(1, NH, head_peer, 0)
    pl.semaphore_wait(bar, NC - 1 + NH - 1)


def run_flows(*flows):
    flows = list(flows)
    while flows:
        for f in list(flows):
            try:
                next(f)
            except StopIteration:
                flows.remove(f)


def start_dispatch(packed, g, asend, arecv, lsem):
    i, h = coords()
    mine = pl.ds(pl.multiple_of(i * CAP, CAP), CAP)

    def send(o, c):
        d = lax.rem(i + o, NC)
        theirs = pl.ds(pl.multiple_of(d * CAP, CAP), CAP)
        remote(packed.at[:, theirs], g.at[h, :, mine], asend.at[o], arecv.at[o], d, h).start()
        return c

    own = pltpu.make_async_copy(packed.at[:, mine], g.at[h, :, mine], lsem)
    own.start()
    lax.fori_loop(1, NC, send, 0)
    own.wait()


def wait_dispatch(packed, g, asend, arecv):
    i, h = coords()

    def one(o, c):
        s = lax.rem(i - o + NC, NC)
        theirs = pl.ds(pl.multiple_of(s * CAP, CAP), CAP)
        remote(packed.at[:, theirs], g.at[h, :, theirs], asend.at[o], arecv.at[o], s, h).wait()
        return c

    lax.fori_loop(1, NC, one, 0)


def gather_flow(g, gate, ssem, rsem):
    i, h = coords()
    xl, y = h // 4, lax.rem(h, 4)
    xp, up, down = head_of(1 - xl, y), head_of(xl, y + 1), head_of(xl, y - 1)
    pup, pdown = head_of(1 - xl, y + 1), head_of(1 - xl, y - 1)
    far, pfar = head_of(xl, y + 2), head_of(1 - xl, y + 2)
    half_rows = ROWS // 2
    chunks = [(e, hf) for hf in range(2) for e in range(2)]

    def copy(kind, c, block, target):
        e, hf = c
        view = g.at[block, e, pl.ds(hf * half_rows, half_rows)]
        n = e * 2 + hf
        return remote(view, view, ssem.at[kind, n], rsem.at[kind, n], i, target)

    gate()
    for c in chunks:
        copy(0, c, h, xp).start()
        copy(1, c, h, up).start()
        copy(2, c, h, down).start()
    yield
    for c in chunks:
        copy(0, c, xp, xp).wait_recv()
        copy(3, c, xp, up).start()
        copy(4, c, xp, down).start()
        yield
        if c[0] == 0:
            copy(1, c, down, up).wait_recv()
            copy(5, c, down, up).start()
        else:
            copy(2, c, up, down).wait_recv()
            copy(5, c, up, down).start()
        yield
    for c in chunks:
        copy(5, c, far, up).wait_recv()
        copy(6, c, far, xp).start()
        yield
    for c in chunks:
        if c[0] == 0:
            copy(2, c, up, up).wait_recv()
        else:
            copy(1, c, down, up).wait_recv()
        copy(3, c, pdown, up).wait_recv()
        copy(4, c, pup, up).wait_recv()
        copy(6, c, pfar, up).wait_recv()
        yield
    for c in chunks:
        copy(0, c, h, xp).wait_send()
        copy(1, c, h, up).wait_send()
        copy(2, c, h, down).wait_send()
        copy(3, c, xp, up).wait_send()
        copy(4, c, xp, down).wait_send()
        copy(5, c, down, up).wait_send()
        copy(6, c, far, xp).wait_send()
    yield


def kv_flow(kv, zs, zr, ks, kr, ps, pr):
    i, h = coords()
    xh, z, core = i // 16, lax.rem(i // 2, 8), lax.rem(i, 2)
    other = ctx_of(1 - xh, z, core)
    up, down = ctx_of(xh, z + 1, core), ctx_of(xh, z - 1, core)
    twin = ctx_of(xh, z, 1 - core)

    def cross(block):
        return remote(kv.at[block], kv.at[block], ps, pr, other, h)

    def ring(k, d, s):
        half = xh if k == 0 else 1 - xh
        block = ctx_of(half, z - s if d == 0 else z + s, core)
        return remote(kv.at[block], kv.at[block], zs.at[k, d, s], zr.at[k, d, s], up if d == 0 else down, h)

    def landed(k, d, s):
        half = xh if k == 0 else 1 - xh
        block = ctx_of(half, z - s - 1 if d == 0 else z + s + 1, core)
        return remote(kv.at[block], kv.at[block], zs.at[k, d, s], zr.at[k, d, s], up if d == 0 else down, h)

    def share(half, dz):
        block = ctx_of(half, z + dz, core)
        n = (0 if half is xh else 8) + dz % 8
        return remote(kv.at[block], kv.at[block], ks.at[n], kr.at[n], twin, h)

    def shared(half, dz):
        block = ctx_of(half, z + dz, 1 - core)
        n = (0 if half is xh else 8) + dz % 8
        return remote(kv.at[block], kv.at[block], ks.at[n], kr.at[n], twin, h)

    halves = (xh, 1 - xh)
    cross(i).start()
    ring(0, 0, 0).start()
    ring(0, 1, 0).start()
    share(halves[0], 0).start()
    yield
    cross(other).wait_recv()
    ring(1, 0, 0).start()
    ring(1, 1, 0).start()
    share(halves[1], 0).start()
    yield
    for s in range(4):
        for k in range(2):
            landed(k, 0, s).wait_recv()
            if s < 3:
                ring(k, 0, s + 1).start()
            share(halves[k], -s - 1).start()
            if s < 3:
                landed(k, 1, s).wait_recv()
                if s < 2:
                    ring(k, 1, s + 1).start()
                share(halves[k], s + 1).start()
            yield
    cross(i).wait_send()
    for k in range(2):
        for s in range(4):
            ring(k, 0, s).wait_send()
        for s in range(3):
            ring(k, 1, s).wait_send()
        for dz in range(-4, 4):
            share(halves[k], dz).wait_send()
            shared(halves[k], dz).wait_recv()
    yield


def routing(ids, cw):
    eio = lax.broadcasted_iota(jnp.int32, (TOK, 2 * NC), 1)
    hot = jnp.zeros((TOK, 2 * NC), F32)
    wts = jnp.zeros((TOK, 2 * NC), F32)
    for k in range(TOP):
        m = ids[:, k : k + 1] == eio
        hot = hot + jnp.where(m, 1.0, 0.0)
        wts = wts + jnp.where(m, cw[:, k : k + 1], 0.0)
    r = lax.broadcasted_iota(jnp.int32, (TOK, TOK), 0)
    c = lax.broadcasted_iota(jnp.int32, (TOK, TOK), 1)
    lower = jnp.where(c < r, 1.0, 0.0).astype(BF)
    earlier = dot(lower, hot.astype(BF))
    n = lax.broadcasted_iota(jnp.int32, (2 * NC, SLOTS), 1)
    e = lax.broadcasted_iota(jnp.int32, (2 * NC, SLOTS), 0)
    spread = jnp.where(e == 2 * (lax.rem(n, ROWS) // CAP) + n // ROWS, 1.0, 0.0).astype(BF)
    hot_n = dot(hot.astype(BF), spread)
    earlier_n = dot(earlier.astype(BF), spread)
    slot = lax.rem(lax.broadcasted_iota(jnp.int32, (TOK, SLOTS), 1), CAP).astype(F32)
    place = jnp.where((hot_n > 0.5) & (earlier_n == slot), 1.0, 0.0)
    hi = wts.astype(BF)
    lo = (wts - hi.astype(F32)).astype(BF)
    whi = place * dot(hi, spread)
    wlo = place * dot(lo, spread)
    return place.astype(BF), whi.astype(BF), wlo.astype(BF)


def kernel_a(k_ref, v_ref, ids_ref, cw_ref, cot_ref, kv, g, place, whi, wlo,
             packed, lsem, zs, zr, ks, kr, ps, pr, asend, arecv, gs, gr):
    i, h = coords()
    greet()
    a = pltpu.make_async_copy(k_ref, kv.at[i, 0], lsem.at[0])
    b = pltpu.make_async_copy(v_ref, kv.at[i, 1], lsem.at[1])
    a.start()
    b.start()
    a.wait()
    b.wait()
    flow = kv_flow(kv, zs, zr, ks, kr, ps, pr)
    next(flow)
    p, hi, lo = routing(ids_ref[...], cw_ref[...])
    place[...] = p
    whi[...] = hi
    wlo[...] = lo
    cot = cot_ref[...]
    rows = dot(hi, cot, 0, 0) + dot(lo, cot, 0, 0)
    packed[...] = rows.astype(BF).reshape(2, ROWS, W)
    start_dispatch(packed, g, asend, arecv, lsem.at[2])
    next(flow)
    run_flows(gather_flow(g, lambda: wait_dispatch(packed, g, asend, arecv), gs, gr), flow)


def exchange_stats(buf, ssem, rsem):
    i, h = coords()
    for o in range(1, NH):
        d = lax.rem(h + o, NH)
        remote(buf.at[0], buf.at[o], ssem.at[o], rsem.at[o], i, d).start()
    total = buf[0]
    for o in range(1, NH):
        d = lax.rem(h + o, NH)
        remote(buf.at[0], buf.at[o], ssem.at[o], rsem.at[o], i, d).wait()
        total = total + buf[o]
    return total


def kernel_b(att, w_ref, res, gain, place, g, normed, inv,
             terms, got, stats, packed, lsem, ts, tr, ss, sr, asend, arecv, gs, gr):
    i, h = coords()
    greet()
    t = dot(att[...], w_ref[...]).astype(BF)
    for d in range(NH):
        terms[d] = t[:, d * W : (d + 1) * W]
    for o in range(1, NH):
        d = lax.rem(h + o, NH)
        remote(terms.at[d], got.at[o], ts.at[o], tr.at[o], i, d).start()
    hidden = terms[h].astype(F32)
    for o in range(1, NH):
        d = lax.rem(h + o, NH)
        remote(terms.at[d], got.at[o], ts.at[o], tr.at[o], i, d).wait()
        hidden = hidden + got[o].astype(F32)
    hidden = hidden + res[...].astype(F32)
    squares = jnp.sum(hidden * hidden, axis=1, keepdims=True)
    stats[0] = jnp.broadcast_to(squares, (TOK, TOK)).T[0:8]
    total = exchange_stats(stats, ss, sr)
    total = jnp.broadcast_to(total[0:1], (TOK, TOK)).T
    inverse = lax.rsqrt(total / D + 1e-06)
    inv[...] = inverse
    nrm = hidden * inverse[:, 0:1]
    normed[...] = nrm
    inputs = (nrm * gain[...]).astype(BF)
    packed[...] = dot(place[...], inputs, 0, 0).astype(BF).reshape(2, ROWS, W)
    start_dispatch(packed, g, asend, arecv, lsem)
    run_flows(gather_flow(g, lambda: wait_dispatch(packed, g, asend, arecv), gs, gr))


def kernel_c(gin, gcot, wg, wu, wd, ids_ref, place, whi, wlo, cot_ref, normed, inv, gain, w_ref,
             moe, attg, resg, gaing, combg, dgate, dup, ddown,
             act_s, gd_s, ud_s, gp_s, up_s, t_ref, r_ref, fin, picked, stats, rgb, gsum,
             lsem, fs, fr, bs, br, ss, sr, rs, rr, qs, qr):
    i, h = coords()
    xl, y = h // 4, lax.rem(h, 4)
    xp, up, down = head_of(1 - xl, y), head_of(xl, y + 1), head_of(xl, y - 1)
    pup, pdown = head_of(1 - xl, y + 1), head_of(1 - xl, y - 1)
    far, pfar = head_of(xl, y + 2), head_of(1 - xl, y + 2)
    HR = ROWS // 2
    greet()

    def rows_of(ref, e, lo, n):
        return jnp.concatenate([ref[b, e, lo : lo + n] for b in range(NH)], axis=1)

    def forward(e, hf):
        sl = slice(hf * HR, (hf + 1) * HR)
        x = rows_of(gin, e, hf * HR, HR)
        gp = dot(x, wg[e], 1, 1)
        u = dot(x, wu[e], 1, 1)
        gp_s[e, sl] = gp
        up_s[e, sl] = u
        act = (gp * jax.nn.sigmoid(gp) * u).astype(BF)
        act_s[e, sl] = act
        for b in range(NH):
            t_ref[0, b, e, sl] = dot(act, wd[e, :, b * W : (b + 1) * W]).astype(BF)

    def backward(e, hf):
        sl = slice(hf * HR, (hf + 1) * HR)
        x = rows_of(gcot, e, hf * HR, HR)
        ag = dot(x, wd[e], 1, 1)
        gp = gp_s[e, sl]
        s = jax.nn.sigmoid(gp)
        gd = (ag * up_s[e, sl] * s * (1.0 + gp * (1.0 - s))).astype(BF)
        ud = (ag * gp * s).astype(BF)
        gd_s[e, sl] = gd
        ud_s[e, sl] = ud
        for b in range(NH):
            cs = slice(b * W, (b + 1) * W)
            t_ref[1, b, e, sl] = (dot(gd, wg[e, :, cs]) + dot(ud, wu[e, :, cs])).astype(BF)

    def weight_grads(e):
        for b in range(NH):
            cs = slice(b * W, (b + 1) * W)
            x = gin[b, e]
            dgate[e, :, cs] = dot(gd_s[e], x, 0, 0).astype(BF)
            dup[e, :, cs] = dot(ud_s[e], x, 0, 0).astype(BF)
            ddown[e, :, cs] = dot(act_s[e], gcot[b, e], 0, 0).astype(BF)

    def tview(f, block):
        t, e, hf = f
        return t_ref.at[t, block, e, pl.ds(hf * HR, HR)]

    def copy(kind, f, block, target):
        n = f[0] * 4 + f[1] * 2 + f[2]
        return remote(tview(f, block), r_ref.at[n, kind], fs.at[kind, n], fr.at[kind, n], i, target)

    def add(f, block, kinds):
        n = f[0] * 4 + f[1] * 2 + f[2]
        v = tview(f, block)
        acc = v[...].astype(F32)
        for kind in kinds:
            acc = acc + r_ref[n, kind].astype(F32)
        return acc.astype(BF)

    def stage0(f):
        copy(0, f, pfar, xp).start()
        copy(1, f, pup, up).start()
        copy(2, f, pdown, down).start()
        if f[2] == 0:
            copy(6, f, down, down).start()
        else:
            copy(5, f, up, up).start()

    def stage1(f):
        copy(0, f, far, xp).wait_recv()
        tview(f, far)[...] = add(f, far, (0,))
        copy(3, f, far, up if f[2] == 0 else down).start()
        copy(1, f, xp, up).wait_recv()
        copy(2, f, xp, up).wait_recv()
        tview(f, xp)[...] = add(f, xp, (1, 2))
        copy(4, f, xp, xp).start()

    def stage2(f):
        block = up if f[2] == 0 else down
        copy(3, f, block, up).wait_recv()
        tview(f, block)[...] = add(f, block, (3,))
        copy(5 if f[2] == 0 else 6, f, block, block).start()

    def stage3(f):
        t, e, hf = f
        for kind in (4, 5, 6):
            copy(kind, f, h, up).wait_recv()
        fin[t, e, hf * HR : (hf + 1) * HR] = add(f, h, (4, 5, 6))

        def send(k, c):
            d = hf * 16 + k

            @pl.when(d != i)
            def _():
                back(t, e, d).start()

            return c

        lax.fori_loop(0, 16, send, 0)

    def back(t, e, d):
        return remote(fin.at[t, e, pl.ds(pl.multiple_of(d * CAP, CAP), CAP)], picked.at[t, e, i],
                      bs.at[t, e], br.at[t, e], d, h)

    def drain(f):
        for kind, block in ((0, pfar), (1, pup), (2, pdown), (3, far), (4, xp), (5, up), (6, down)):
            copy(kind, f, block, xp).wait_send()

    flows = [(t, e, hf) for t in range(2) for e in range(2) for hf in range(2)]
    for n in range(len(flows) + 3):
        if n < len(flows):
            t, e, hf = flows[n]
            (forward if t == 0 else backward)(e, hf)
            stage0(flows[n])
        elif n == len(flows):
            weight_grads(0)
        elif n == len(flows) + 1:
            weight_grads(1)
        if 0 <= n - 1 < len(flows):
            stage1(flows[n - 1])
        if 0 <= n - 2 < len(flows):
            stage2(flows[n - 2])
        if 0 <= n - 3 < len(flows):
            stage3(flows[n - 3])

    def landed(t):
        mine = pl.ds(pl.multiple_of(i * CAP, CAP), CAP)
        for e in range(2):
            own = pltpu.make_async_copy(fin.at[t, e, mine], picked.at[t, e, i], lsem)
            own.start()
            own.wait()
            part = picked.at[t, e, pl.ds(0, NC - 1)]
            remote(part, part, bs.at[t, e], br.at[t, e], i, xp).wait()
        return picked[t].reshape(SLOTS, W)

    rows = landed(0)
    hi, lo = whi[...], wlo[...]
    moe[...] = (dot(hi, rows) + dot(lo, rows)).astype(BF)
    every = dot(cot_ref[...], rows, 1, 1)
    pl_f = place[...].astype(F32)
    every = every * pl_f
    n = lax.broadcasted_iota(jnp.int32, (TOK, SLOTS), 1)
    expert = 2 * (lax.rem(n, ROWS) // CAP) + n // ROWS
    ids = ids_ref[...]
    lane = lax.broadcasted_iota(jnp.int32, (TOK, TOK), 1)
    packed = jnp.zeros((TOK, TOK), F32)
    for k in range(TOP):
        term = jnp.sum(jnp.where(expert == ids[:, k : k + 1], every, 0.0), axis=1, keepdims=True)
        packed = jnp.where(lane == k, term, packed)

    rows = landed(1)
    input_grad = dot(place[...], rows)
    nrm = normed[...]
    gsum[0] = jnp.broadcast_to(jnp.sum(input_grad * nrm, axis=0, keepdims=True), (8, W))

    def gain_copy(o):
        d = lax.rem(i + o, NC)
        return remote(gsum.at[0], gsum.at[o], qs.at[o], qr.at[o], d, h)

    def gain_start(o, c):
        gain_copy(o).start()
        return c

    ng = input_grad * gain[...]
    packed = jnp.where(lane == TOP, jnp.sum(ng * nrm, axis=1, keepdims=True), packed)
    stats[0] = packed.T[0:8]
    total = exchange_stats(stats, ss, sr)
    lax.fori_loop(1, NC, gain_start, 0)
    total = jnp.concatenate([total, jnp.zeros((TOK - 8, TOK), F32)], axis=0).T
    combg[...] = total[:, 0:TOP]
    centre = total[:, TOP : TOP + 1] / D
    rg = (inv[:, 0:1] * (ng - nrm * centre)).astype(BF)
    resg[...] = rg
    rgb[h] = rg
    for o in range(1, NH):
        d = lax.rem(h + o, NH)
        remote(rgb.at[h], rgb.at[h], rs.at[o], rr.at[o], i, d).start()
    for o in range(1, NH):
        s = lax.rem(h - o + NH, NH)
        remote(rgb.at[s], rgb.at[s], rs.at[o], rr.at[o], i, s).wait()
    whole = jnp.concatenate([rgb[b] for b in range(NH)], axis=1)
    attg[...] = dot(whole, w_ref[...], 1, 1).astype(BF)

    def gain_wait(o, c):
        gain_copy(o).wait()
        return c + gsum[o]

    gaing[...] = lax.fori_loop(1, NC, gain_wait, gsum[0])
    for f in flows:
        drain(f)


VM = pl.BlockSpec(memory_space=pltpu.VMEM)
ANY = pl.BlockSpec(memory_space=pl.ANY)
DMA = pltpu.SemaphoreType.DMA
SDS = jax.ShapeDtypeStruct


def params(n, mib):
    return pltpu.CompilerParams(collective_id=n, has_side_effects=True, vmem_limit_bytes=mib << 20)


def gather_sems():
    return [DMA((NC,)), DMA((NC,)), DMA((7, 4)), DMA((7, 4))]


def call_a(k, v, ids, cw, cot):
    return pl.pallas_call(
        kernel_a,
        out_shape=(
            SDS((NC, 2, TOK, W), BF),
            SDS((NH, 2, ROWS, W), BF),
            SDS((TOK, SLOTS), BF),
            SDS((TOK, SLOTS), BF),
            SDS((TOK, SLOTS), BF),
        ),
        in_specs=[VM] * 5,
        out_specs=(ANY, ANY, VM, VM, VM),
        scratch_shapes=[
            pltpu.VMEM((2, ROWS, W), BF),
            DMA((3,)),
            DMA((2, 2, 4)), DMA((2, 2, 4)), DMA((16,)), DMA((16,)), DMA, DMA,
            *gather_sems(),
        ],
        compiler_params=params(1, 40),
        name="gather_keys_place_cotangents",
    )(k, v, ids, cw, cot)


def call_b(att, w, res, gain, place):
    return pl.pallas_call(
        kernel_b,
        out_shape=(SDS((NH, 2, ROWS, W), BF), SDS((TOK, W), F32), SDS((TOK, TOK), F32)),
        in_specs=[VM] * 5,
        out_specs=(ANY, VM, VM),
        scratch_shapes=[
            pltpu.VMEM((NH, TOK, W), BF),
            pltpu.VMEM((NH, TOK, W), BF),
            pltpu.VMEM((NH, 8, TOK), F32),
            pltpu.VMEM((2, ROWS, W), BF),
            DMA,
            DMA((NH,)), DMA((NH,)), DMA((NH,)), DMA((NH,)),
            *gather_sems(),
        ],
        compiler_params=params(2, 40),
        name="project_norm_place",
    )(att, w, res, gain, place)


def call_c(*args):
    return pl.pallas_call(
        kernel_c,
        out_shape=(
            SDS((TOK, W), BF), SDS((TOK, W), BF), SDS((TOK, W), BF), SDS((8, W), F32), SDS((TOK, TOP), F32),
            SDS((2, FD, D), BF), SDS((2, FD, D), BF), SDS((2, FD, D), BF),
        ),
        in_specs=[VM] * 14,
        out_specs=(VM,) * 8,
        scratch_shapes=[
            pltpu.VMEM((2, ROWS, FD), BF), pltpu.VMEM((2, ROWS, FD), BF), pltpu.VMEM((2, ROWS, FD), BF),
            pltpu.VMEM((2, ROWS, FD), F32), pltpu.VMEM((2, ROWS, FD), F32),
            pltpu.VMEM((2, NH, 2, ROWS, W), BF),
            pltpu.VMEM((8, 7, ROWS // 2, W), BF),
            pltpu.VMEM((2, 2, ROWS, W), BF),
            pltpu.VMEM((2, 2, NC, CAP, W), BF),
            pltpu.VMEM((NH, 8, TOK), F32),
            pltpu.VMEM((NH, TOK, W), BF),
            pltpu.VMEM((NC, 8, W), F32),
            DMA,
            DMA((7, 8)), DMA((7, 8)), DMA((2, 2)), DMA((2, 2)),
            DMA((NH,)), DMA((NH,)), DMA((NH,)), DMA((NH,)), DMA((NC,)), DMA((NC,)),
        ],
        compiler_params=params(3, 58),
        name="experts_reduce_return",
    )(*args)


def attend(q, kv, i):
    outs = []
    pos = i * TOK + jnp.arange(TOK, dtype=jnp.int32)
    allowed = pos[:, None] >= jnp.arange(NC * TOK, dtype=jnp.int32)[None, :]
    for n in range(2):
        cs = slice(n * DH, (n + 1) * DH)
        k = kv[:, 0, :, cs].reshape(NC * TOK, DH)
        v = kv[:, 1, :, cs].reshape(NC * TOK, DH)
        s = jnp.dot(q[:, cs], k.T, preferred_element_type=F32) * DH ** (-0.5)
        top = jnp.max(jnp.where(allowed, s, -1e30), axis=1, keepdims=True)
        wts = jnp.where(allowed, jnp.exp(s - top), 0.0)
        tot = jnp.sum(wts, axis=1, keepdims=True)
        outs.append(jnp.dot(wts.astype(BF), v, preferred_element_type=F32) / tot)
    return jnp.concatenate(outs, axis=1).astype(BF)


def per_device(queries, key_rows, value_rows, output_weight, residual_stream, norm_gain, expert_ids,
               combine_weights, gate_weight, up_weight, down_weight, cotangent):
    i = lax.axis_index("ctx")
    gain = norm_gain.reshape(1, W)
    kv, gcot, place, whi, wlo = call_a(key_rows, value_rows, expert_ids, combine_weights, cotangent)
    att = attend(queries, kv, i)
    gin, normed, inv = call_b(att, output_weight, residual_stream, gain, place)
    moe, attg, resg, gaing, combg, dgate, dup, ddown = call_c(
        gin, gcot, gate_weight, up_weight, down_weight, expert_ids, place, whi, wlo, cotangent,
        normed, inv, gain, output_weight)
    return moe, attg, resg, gaing[0], combg, dgate, dup, ddown


def solution(mesh):
    return jax.shard_map(
        per_device,
        mesh=mesh,
        in_specs=(
            P("ctx", "head"), P("ctx", "head"), P("ctx", "head"), P("head", None), P("ctx", "head"), P("head"),
            P("ctx", None), P("ctx", None), P("ctx", "head", None), P("ctx", "head", None),
            P("ctx", "head", None), P("ctx", "head"),
        ),
        out_specs=(
            P("ctx", "head"), P("ctx", "head"), P("ctx", "head"), P("head"), P("ctx", None),
            P("ctx", "head", None), P("ctx", "head", None), P("ctx", "head", None),
        ),
        check_vma=False,
    )
```

```python
import jax
import jax.numpy as jnp
from jax import lax
from jax.experimental import pallas as pl
from jax.experimental.pallas import tpu as pltpu
from jax.sharding import PartitionSpec as P

D = 2048
TOP = 6
DH = 128
NC = 32
NH = 8
TOK = 128
W = 256
FD = 176
CAP = 16
ROWS = NC * CAP
SLOTS = 2 * ROWS
MESH = pl.DeviceIdType.MESH
BF = jnp.bfloat16
F32 = jnp.float32


def dot(a, b, ca=1, cb=0):
    return lax.dot_general(a, b, (((ca,), (cb,)), ((), ())), preferred_element_type=F32)


def coords():
    return lax.axis_index("ctx"), lax.axis_index("head")


def head_of(xl, y):
    return xl * 4 + lax.rem(y + 4, 4)


def ctx_of(xh, z, core):
    return xh * 16 + lax.rem(z + 8, 8) * 2 + core


def remote(src, dst, ssem, rsem, ctx, head):
    return pltpu.make_async_remote_copy(
        src, dst, ssem, rsem, device_id=(ctx, head), device_id_type=MESH
    )


def greet():
    i, h = coords()
    bar = pltpu.get_barrier_semaphore()

    def ctx_peer(o, c):
        pl.semaphore_signal(bar, 1, device_id=(lax.rem(i + o, NC), h), device_id_type=MESH)
        return c

    def head_peer(o, c):
        pl.semaphore_signal(bar, 1, device_id=(i, lax.rem(h + o, NH)), device_id_type=MESH)
        return c

    lax.fori_loop(1, NC, ctx_peer, 0)
    lax.fori_loop(1, NH, head_peer, 0)
    pl.semaphore_wait(bar, NC - 1 + NH - 1)


def routing(ids, cw):
    eio = lax.broadcasted_iota(jnp.int32, (TOK, 2 * NC), 1)
    hot = jnp.zeros((TOK, 2 * NC), F32)
    wts = jnp.zeros((TOK, 2 * NC), F32)
    for k in range(TOP):
        m = ids[:, k : k + 1] == eio
        hot = hot + jnp.where(m, 1.0, 0.0)
        wts = wts + jnp.where(m, cw[:, k : k + 1], 0.0)
    r = lax.broadcasted_iota(jnp.int32, (TOK, TOK), 0)
    c = lax.broadcasted_iota(jnp.int32, (TOK, TOK), 1)
    lower = jnp.where(c < r, 1.0, 0.0).astype(BF)
    earlier = dot(lower, hot.astype(BF))
    n = lax.broadcasted_iota(jnp.int32, (2 * NC, SLOTS), 1)
    e = lax.broadcasted_iota(jnp.int32, (2 * NC, SLOTS), 0)
    spread = jnp.where(e == 2 * (lax.rem(n, ROWS) // CAP) + n // ROWS, 1.0, 0.0).astype(BF)
    hot_n = dot(hot.astype(BF), spread)
    earlier_n = dot(earlier.astype(BF), spread)
    slot = lax.rem(lax.broadcasted_iota(jnp.int32, (TOK, SLOTS), 1), CAP).astype(F32)
    place = jnp.where((hot_n > 0.5) & (earlier_n == slot), 1.0, 0.0)
    hi = wts.astype(BF)
    lo = (wts - hi.astype(F32)).astype(BF)
    whi = place * dot(hi, spread)
    wlo = place * dot(lo, spread)
    return place.astype(BF), whi.astype(BF), wlo.astype(BF)


def start_dispatch(packed, g, asend, arecv, lsem):
    i, h = coords()
    mine = pl.ds(pl.multiple_of(i * CAP, CAP), CAP)

    for e in range(2):

        def send(o, c):
            d = lax.rem(i + o, NC)
            theirs = pl.ds(pl.multiple_of(d * CAP, CAP), CAP)
            remote(packed.at[e, theirs], g.at[h, e, mine], asend.at[e], arecv.at[e], d, h).start()
            return c

        lax.fori_loop(1, NC, send, 0)
    own = pltpu.make_async_copy(packed.at[:, mine], g.at[h, :, mine], lsem)
    own.start()
    own.wait()


def dispatched(packed, g, asend, arecv, e):
    i, h = coords()
    most = pl.ds(0, (NC - 1) * CAP)
    return remote(packed.at[e, most], g.at[h, e, most], asend.at[e], arecv.at[e], i, 7 - h)


def gather_flow(g, gate, ssem, rsem, done):
    i, h = coords()
    xl, y = h // 4, lax.rem(h, 4)
    xp, up, down = head_of(1 - xl, y), head_of(xl, y + 1), head_of(xl, y - 1)
    pup, pdown = head_of(1 - xl, y + 1), head_of(1 - xl, y - 1)
    far, pfar = head_of(xl, y + 2), head_of(1 - xl, y + 2)
    half_rows = ROWS // 2
    chunks = [(e, hf) for e in range(2) for hf in range(2)]

    def copy(kind, c, block, target):
        e, hf = c
        view = g.at[block, e, pl.ds(hf * half_rows, half_rows)]
        n = e * 2 + hf
        return remote(view, view, ssem.at[kind, n], rsem.at[kind, n], i, target)

    def own(n):
        e, hf = chunks[n]
        if hf == 0:
            gate(e)
        copy(0, chunks[n], h, xp).start()
        copy(1, chunks[n], h, up).start()
        copy(2, chunks[n], h, down).start()

    own(0)
    for n in range(7):
        if n + 1 < 4:
            own(n + 1)
        yield
        if 0 <= n < 4:
            c = chunks[n]
            copy(0, c, xp, xp).wait_recv()
            copy(3, c, xp, up).start()
            copy(4, c, xp, down).start()
            if c[1] == 0:
                copy(1, c, down, up).wait_recv()
                copy(5, c, down, up).start()
            else:
                copy(2, c, up, down).wait_recv()
                copy(5, c, up, down).start()
        if 0 <= n - 1 < 4:
            c = chunks[n - 1]
            copy(5, c, far, up).wait_recv()
            copy(6, c, far, xp).start()
        if 0 <= n - 2 < 4:
            c = chunks[n - 2]
            if c[1] == 0:
                copy(2, c, up, up).wait_recv()
            else:
                copy(1, c, down, up).wait_recv()
            copy(3, c, pdown, up).wait_recv()
            copy(4, c, pup, up).wait_recv()
            copy(6, c, pfar, up).wait_recv()
            done(n - 2)
    for c in chunks:
        copy(0, c, h, xp).wait_send()
        copy(1, c, h, up).wait_send()
        copy(2, c, h, down).wait_send()
        copy(3, c, xp, up).wait_send()
        copy(4, c, xp, down).wait_send()
        copy(5, c, down, up).wait_send()
        copy(6, c, far, xp).wait_send()


def key_flow(kv, zs, zr, ks, kr):
    i, h = coords()
    xh, z, core = i // 16, lax.rem(i // 2, 8), lax.rem(i, 2)
    up, down = ctx_of(xh, z + 1, core), ctx_of(xh, z - 1, core)
    twin = ctx_of(xh, z, 1 - core)
    lanes = [(k, d) for k in range(2) for d in range(2)]

    def hops(k, d):
        return 4 if k == d else 3

    def view(k, dz, c):
        return kv.at[lax.rem(z + dz + 8, 8) * 2 + c, k]

    def ring(k, d, s):
        v = view(k, -s if d == 0 else s, core)
        return remote(v, v, zs.at[k, d, s], zr.at[k, d, s], up if d == 0 else down, h)

    def landed(k, d, s):
        v = view(k, -s - 1 if d == 0 else s + 1, core)
        return remote(v, v, zs.at[k, d, s], zr.at[k, d, s], up if d == 0 else down, h)

    def share(k, dz, c):
        v = view(k, dz, c)
        return remote(v, v, ks.at[k, dz % 8], kr.at[k, dz % 8], twin, h)

    for k, d in lanes:
        ring(k, d, 0).start()
    for k in range(2):
        share(k, 0, core).start()
    yield
    for s in range(4):
        for k, d in lanes:
            if s < hops(k, d):
                landed(k, d, s).wait_recv()
                if s + 1 < hops(k, d):
                    ring(k, d, s + 1).start()
                share(k, -s - 1 if d == 0 else s + 1, core).start()
        yield
    for k in range(2):
        for dz in range(-4, 4):
            share(k, dz, 1 - core).wait_recv()
    yield
    for k, d in lanes:
        for s in range(hops(k, d)):
            ring(k, d, s).wait_send()
    for k in range(2):
        for dz in range(-4, 4):
            share(k, dz, core).wait_send()
    yield


def to_rows(columns):
    lane = lax.broadcasted_iota(jnp.int32, (TOK, TOK), 1)
    packed = jnp.zeros((TOK, TOK), F32)
    for k, c in enumerate(columns):
        packed = jnp.where(lane == k, c, packed)
    return packed.T[0:8]


def to_columns(rows):
    return jnp.concatenate([rows, jnp.zeros((TOK - 8, TOK), F32)], axis=0).T


def layer_kernel(q_in, k_in, v_in, w_in, res_in, gain, ids_in, cw_in, wg_in, wu_in, wd_in, cot_in,
                 moe_out, attg_out, resg_out, gaing_out, combg_out, dgate_out, dup_out, ddown_out,
                 qb, kv, w_ref, res, ids_ref, cw_ref, wg, wu, wd, cot_ref,
                 place, whi, wlo, packed, gcot, gin, ob, os, terms, got, stats, stats2, normed, inv,
                 act_s, gd_s, ud_s, gp_s, up_s, t_ref, r_ref, fin, picked, rgb, gsum,
                 moe, attg, resg, gaing, combg, dgate, dup, ddown,
                 lsem, osem, zs, zr, ks, kr, xs, xr, asend, arecv, gs, gr, ts, tr, ss, sr,
                 fs, fr, bs, br, rs, rr, qs, qr):
    i, h = coords()
    xh, z, core = i // 16, lax.rem(i // 2, 8), lax.rem(i, 2)
    xl, y = h // 4, lax.rem(h, 4)
    xp, up, down = head_of(1 - xl, y), head_of(xl, y + 1), head_of(xl, y - 1)
    pup, pdown = head_of(1 - xl, y + 1), head_of(1 - xl, y - 1)
    far, pfar = head_of(xl, y + 2), head_of(1 - xl, y + 2)
    other = ctx_of(1 - xh, z, core)
    HR = ROWS // 2
    seat = lax.rem(i, 16)

    loads = [
        pltpu.make_async_copy(s, d, lsem.at[n])
        for n, (s, d) in enumerate((
            (k_in, kv.at[seat, 0]), (v_in, kv.at[seat, 1]), (q_in, qb.at[0]), (ids_in, ids_ref), (cw_in, cw_ref),
            (cot_in, cot_ref), (w_in, w_ref), (res_in, res), (wg_in, wg), (wu_in, wu), (wd_in, wd),
        ))
    ]
    for c in loads:
        c.start()
    greet()
    for c in loads[0:3]:
        c.wait()

    keys = key_flow(kv, zs, zr, ks, kr)
    next(keys)
    q_swap = remote(qb.at[0], qb.at[1], xs.at[0], xr.at[0], other, h)
    q_swap.start()
    for c in loads[3:6]:
        c.wait()
    pad = jnp.zeros((TOK - TOP, TOK), F32)
    ids = jnp.concatenate([ids_ref[...].astype(F32), pad], axis=0).T.astype(jnp.int32)
    cw = jnp.concatenate([cw_ref[...], pad], axis=0).T
    p, hi, lo = routing(ids, cw)
    place[...] = p
    whi[...] = hi
    wlo[...] = lo
    next(keys)
    cot = cot_ref[...]
    rows = dot(hi, cot, 0, 0) + dot(lo, cot, 0, 0)
    packed[0] = rows.astype(BF).reshape(2, ROWS, W)
    next(keys)
    next(keys)
    start_dispatch(packed.at[0], gcot, asend.at[0], arecv.at[0], lsem.at[11])
    next(keys)
    next(keys)

    q_swap.wait_recv()
    q2 = jnp.concatenate([qb[0], qb[1]], axis=0)
    r = lax.broadcasted_iota(jnp.int32, (2 * TOK, 1), 0)
    limit = jnp.where(r < TOK, seat * TOK + r, jnp.where(xh == 0, 16 * TOK - 1, -1))
    allowed = lax.broadcasted_iota(jnp.int32, (2 * TOK, 16 * TOK), 1) <= limit
    outs, tops, sums = [], [], []
    for n in range(2):
        cs = slice(n * DH, (n + 1) * DH)
        s = dot(q2[:, cs], kv[:, 0, :, cs].reshape(16 * TOK, DH), 1, 1) * DH ** (-0.5)
        s = jnp.where(allowed, s, -1e30)
        m = jnp.max(s, axis=1, keepdims=True)
        wts = jnp.exp(s - m)
        tot = jnp.sum(wts, axis=1, keepdims=True)
        o = dot(wts.astype(BF), kv[:, 1, :, cs].reshape(16 * TOK, DH)) / tot
        outs.append(o)
        tops.append(m)
        sums.append(tot)
    seen = jnp.where(xh == 0, 1.0, 0.0)
    ob[0] = jnp.concatenate([o[TOK:] for o in outs], axis=1).astype(BF)
    os[0] = to_rows([tops[0][TOK:], sums[0][TOK:] * seen, tops[1][TOK:], sums[1][TOK:] * seen])
    o_swap = remote(ob.at[0], ob.at[1], xs.at[1], xr.at[1], other, h)
    s_swap = remote(os.at[0], os.at[1], xs.at[2], xr.at[2], other, h)
    o_swap.start()
    s_swap.start()
    loads[6].wait()
    loads[7].wait()
    s_swap.wait_recv()
    o_swap.wait_recv()
    there = to_columns(os[1])
    att = []
    for n in range(2):
        m1, l1 = tops[n][:TOK], sums[n][:TOK]
        m2, l2 = there[:, 2 * n : 2 * n + 1], there[:, 2 * n + 1 : 2 * n + 2]
        m = jnp.maximum(m1, m2)
        a1, a2 = l1 * jnp.exp(m1 - m), l2 * jnp.exp(m2 - m)
        o2 = ob[1, :, n * DH : (n + 1) * DH].astype(F32)
        att.append((a1 * outs[n][:TOK] + a2 * o2) / (a1 + a2))
    att = jnp.concatenate(att, axis=1).astype(BF)

    t = dot(att, w_ref[...]).astype(BF)
    for d in range(NH):
        terms[d] = t[:, d * W : (d + 1) * W]
    for o in range(1, NH):
        d = lax.rem(h + o, NH)
        remote(terms.at[d], got.at[o], ts.at[o], tr.at[o], i, d).start()

    cots = gather_flow(gcot, lambda e: dispatched(packed.at[0], gcot, asend.at[0], arecv.at[0], e).wait_recv(),
                       gs.at[0], gr.at[0], lambda n: None)
    next(cots)
    hidden = res[...].astype(F32) + terms[h].astype(F32)
    for o in range(1, NH):
        d = lax.rem(h + o, NH)
        remote(terms.at[d], got.at[o], ts.at[o], tr.at[o], i, d).wait()
        hidden = hidden + got[o].astype(F32)
    stats[0] = to_rows([jnp.sum(hidden * hidden, axis=1, keepdims=True)])
    for o in range(1, NH):
        remote(stats.at[0], stats.at[o], ss.at[0, o], sr.at[0, o], i, lax.rem(h + o, NH)).start()
    next(cots)
    total = stats[0]
    for o in range(1, NH):
        remote(stats.at[0], stats.at[o], ss.at[0, o], sr.at[0, o], i, lax.rem(h + o, NH)).wait()
        total = total + stats[o]
    inverse = lax.rsqrt(to_columns(total)[:, 0:1] / D + 1e-06)
    inv[...] = jnp.broadcast_to(inverse, (TOK, TOK))
    nrm = hidden * inverse
    normed[...] = nrm
    inputs = (nrm * gain[...]).astype(BF)
    packed[1] = dot(place[...], inputs, 0, 0).astype(BF).reshape(2, ROWS, W)
    start_dispatch(packed.at[1], gin, asend.at[1], arecv.at[1], lsem.at[11])
    for _ in cots:
        pass
    for c in loads[8:]:
        c.wait()

    def rows_of(ref, e, lo, n):
        return jnp.concatenate([ref[b, e, lo : lo + n] for b in range(NH)], axis=1)

    def forward(e, hf):
        sl = slice(hf * HR, (hf + 1) * HR)
        x = rows_of(gin, e, hf * HR, HR)
        gp = dot(x, wg[e], 1, 1)
        u = dot(x, wu[e], 1, 1)
        gp_s[e, sl] = gp
        up_s[e, sl] = u
        act = (gp * jax.nn.sigmoid(gp) * u).astype(BF)
        act_s[e, sl] = act
        for b in range(NH):
            t_ref[0, b, e, sl] = dot(act, wd[e, :, b * W : (b + 1) * W]).astype(BF)

    def backward(e, hf):
        sl = slice(hf * HR, (hf + 1) * HR)
        x = rows_of(gcot, e, hf * HR, HR)
        ag = dot(x, wd[e], 1, 1)
        gp = gp_s[e, sl]
        s = jax.nn.sigmoid(gp)
        gd = (ag * up_s[e, sl] * s * (1.0 + gp * (1.0 - s))).astype(BF)
        ud = (ag * gp * s).astype(BF)
        gd_s[e, sl] = gd
        ud_s[e, sl] = ud
        for b in range(NH):
            cs = slice(b * W, (b + 1) * W)
            t_ref[1, b, e, sl] = (dot(gd, wg[e, :, cs]) + dot(ud, wu[e, :, cs])).astype(BF)

    def weight_grads(e):
        for b in range(NH):
            cs = slice(b * W, (b + 1) * W)
            x = gin[b, e]
            dgate[e, :, cs] = dot(gd_s[e], x, 0, 0).astype(BF)
            dup[e, :, cs] = dot(ud_s[e], x, 0, 0).astype(BF)
            ddown[e, :, cs] = dot(act_s[e], gcot[b, e], 0, 0).astype(BF)

    def tview(f, block):
        t, e, hf = f
        return t_ref.at[t, block, e, pl.ds(hf * HR, HR)]

    def copy(kind, f, block, target):
        n = f[0] * 4 + f[1] * 2 + f[2]
        return remote(tview(f, block), r_ref.at[n, kind], fs.at[kind, n], fr.at[kind, n], i, target)

    def add(f, block, kinds):
        n = f[0] * 4 + f[1] * 2 + f[2]
        v = tview(f, block)
        acc = v[...].astype(F32)
        for kind in kinds:
            acc = acc + r_ref[n, kind].astype(F32)
        return acc.astype(BF)

    def stage0(f):
        copy(0, f, pfar, xp).start()
        copy(1, f, pup, up).start()
        copy(2, f, pdown, down).start()
        if f[2] == 0:
            copy(6, f, down, down).start()
        else:
            copy(5, f, up, up).start()

    def stage1(f):
        copy(0, f, far, xp).wait_recv()
        tview(f, far)[...] = add(f, far, (0,))
        copy(3, f, far, up if f[2] == 0 else down).start()
        copy(1, f, xp, up).wait_recv()
        copy(2, f, xp, up).wait_recv()
        tview(f, xp)[...] = add(f, xp, (1, 2))
        copy(4, f, xp, xp).start()

    def stage2(f):
        block = up if f[2] == 0 else down
        copy(3, f, block, up).wait_recv()
        tview(f, block)[...] = add(f, block, (3,))
        copy(5 if f[2] == 0 else 6, f, block, block).start()

    def stage3(f):
        t, e, hf = f
        for kind in (4, 5, 6):
            copy(kind, f, h, up).wait_recv()
        fin[t, e, hf * HR : (hf + 1) * HR] = add(f, h, (4, 5, 6))

        def send(k, c):
            d = hf * 16 + k

            @pl.when(d != i)
            def _():
                back(t, e, d).start()

            return c

        lax.fori_loop(0, 16, send, 0)

    def back(t, e, d):
        return remote(fin.at[t, e, pl.ds(pl.multiple_of(d * CAP, CAP), CAP)], picked.at[t, e, i],
                      bs.at[t, e], br.at[t, e], d, h)

    def drain(f):
        for kind, block in ((0, pfar), (1, pup), (2, pdown), (3, far), (4, xp), (5, up), (6, down)):
            copy(kind, f, block, xp).wait_send()

    flows = [(t, e, hf) for t in range(2) for e in range(2) for hf in range(2)]
    outward = [
        pltpu.make_async_copy(s, d, osem.at[n])
        for n, (s, d) in enumerate((
            (moe, moe_out), (attg, attg_out), (resg, resg_out), (gaing, gaing_out), (combg, combg_out),
            (dgate, dgate_out), (dup, dup_out), (ddown, ddown_out),
        ))
    ]

    def tick(n):
        if n < len(flows):
            t, e, hf = flows[n]
            (forward if t == 0 else backward)(e, hf)
            stage0(flows[n])
        elif n == len(flows):
            weight_grads(0)
        elif n == len(flows) + 1:
            weight_grads(1)
            for c in outward[5:]:
                c.start()
        if 0 <= n - 1 < len(flows):
            stage1(flows[n - 1])
        if 0 <= n - 2 < len(flows):
            stage2(flows[n - 2])
        if 0 <= n - 3 < len(flows):
            stage3(flows[n - 3])

    for _ in gather_flow(gin, lambda e: dispatched(packed.at[1], gin, asend.at[1], arecv.at[1], e).wait_recv(),
                         gs.at[1], gr.at[1], tick):
        pass
    for n in range(4, len(flows) + 3):
        tick(n)

    def landed(t):
        mine = pl.ds(pl.multiple_of(i * CAP, CAP), CAP)
        for e in range(2):
            own = pltpu.make_async_copy(fin.at[t, e, mine], picked.at[t, e, i], lsem.at[11])
            own.start()
            own.wait()
            part = picked.at[t, e, pl.ds(0, NC - 1)]
            remote(part, part, bs.at[t, e], br.at[t, e], i, xp).wait()
        return picked[t].reshape(SLOTS, W)

    rows = landed(0)
    moe[...] = (dot(whi[...], rows) + dot(wlo[...], rows)).astype(BF)
    outward[0].start()
    every = dot(cot_ref[...], rows, 1, 1) * place[...].astype(F32)
    n = lax.broadcasted_iota(jnp.int32, (TOK, SLOTS), 1)
    expert = 2 * (lax.rem(n, ROWS) // CAP) + n // ROWS
    columns = [
        jnp.sum(jnp.where(expert == ids[:, k : k + 1], every, 0.0), axis=1, keepdims=True) for k in range(TOP)
    ]

    rows = landed(1)
    input_grad = dot(place[...], rows)
    nrm = normed[...]
    gsum[0] = jnp.broadcast_to(jnp.sum(input_grad * nrm, axis=0, keepdims=True), (8, W))

    def gain_copy(o):
        d = lax.rem(i + o, NC)
        return remote(gsum.at[0], gsum.at[o], qs.at[o], qr.at[o], d, h)

    def gain_start(o, c):
        gain_copy(o).start()
        return c

    ng = input_grad * gain[...]
    stats2[0] = to_rows(columns + [jnp.sum(ng * nrm, axis=1, keepdims=True)])
    for o in range(1, NH):
        remote(stats2.at[0], stats2.at[o], ss.at[1, o], sr.at[1, o], i, lax.rem(h + o, NH)).start()
    lax.fori_loop(1, NC, gain_start, 0)
    total = stats2[0]
    for o in range(1, NH):
        remote(stats2.at[0], stats2.at[o], ss.at[1, o], sr.at[1, o], i, lax.rem(h + o, NH)).wait()
        total = total + stats2[o]
    combg[...] = total[0:TOP]
    outward[4].start()
    centre = to_columns(total)[:, TOP : TOP + 1] / D
    rg = (inv[:, 0:1] * (ng - nrm * centre)).astype(BF)
    resg[...] = rg
    outward[2].start()
    rgb[h] = rg
    for o in range(1, NH):
        d = lax.rem(h + o, NH)
        remote(rgb.at[h], rgb.at[h], rs.at[o], rr.at[o], i, d).start()

    def gain_wait(o, c):
        gain_copy(o).wait()
        return c + gsum[o]

    gaing[...] = lax.fori_loop(1, NC, gain_wait, gsum[0])[0:1]
    outward[3].start()
    for f in flows:
        drain(f)
    for part in range(2):
        for e in range(2):
            dispatched(packed.at[part], (gcot, gin)[part], asend.at[part], arecv.at[part], e).wait_send()
    q_swap.wait_send()
    o_swap.wait_send()
    s_swap.wait_send()
    for _ in keys:
        pass
    for o in range(1, NH):
        s = lax.rem(h - o + NH, NH)
        remote(rgb.at[s], rgb.at[s], rs.at[o], rr.at[o], i, s).wait()
    whole = jnp.concatenate([rgb[b] for b in range(NH)], axis=1)
    attg[...] = dot(whole, w_ref[...], 1, 1).astype(BF)
    outward[1].start()
    for c in outward:
        c.wait()


VM = pl.BlockSpec(memory_space=pltpu.VMEM)
ANY = pl.BlockSpec(memory_space=pl.ANY)
DMA = pltpu.SemaphoreType.DMA
SDS = jax.ShapeDtypeStruct
RESULTS = (
    ((TOK, W), BF), ((TOK, W), BF), ((TOK, W), BF), ((1, W), F32), ((TOP, TOK), F32),
    ((2, FD, D), BF), ((2, FD, D), BF), ((2, FD, D), BF),
)


def call_layer(*args):
    v = pltpu.VMEM
    return pl.pallas_call(
        layer_kernel,
        out_shape=tuple(SDS(s, t) for s, t in RESULTS),
        in_specs=[ANY] * 5 + [VM] + [ANY] * 6,
        out_specs=(ANY,) * 8,
        scratch_shapes=[
            v((2, TOK, W), BF), v((16, 2, TOK, W), BF), v((W, D), BF), v((TOK, W), BF),
            v((TOP, TOK), jnp.int32), v((TOP, TOK), F32),
            v((2, FD, D), BF), v((2, FD, D), BF), v((2, FD, D), BF), v((TOK, W), BF),
            v((TOK, SLOTS), BF), v((TOK, SLOTS), BF), v((TOK, SLOTS), BF),
            v((2, 2, ROWS, W), BF), v((NH, 2, ROWS, W), BF), v((NH, 2, ROWS, W), BF),
            v((2, TOK, W), BF), v((2, 8, TOK), F32), v((NH, TOK, W), BF), v((NH, TOK, W), BF),
            v((NH, 8, TOK), F32), v((NH, 8, TOK), F32), v((TOK, W), F32), v((TOK, TOK), F32),
            v((2, ROWS, FD), BF), v((2, ROWS, FD), BF), v((2, ROWS, FD), BF),
            v((2, ROWS, FD), F32), v((2, ROWS, FD), F32),
            v((2, NH, 2, ROWS, W), BF), v((8, 7, ROWS // 2, W), BF), v((2, 2, ROWS, W), BF),
            v((2, 2, NC, CAP, W), BF), v((NH, TOK, W), BF), v((NC, 8, W), F32),
            *[v(s, t) for s, t in RESULTS],
            DMA((12,)), DMA((8,)),
            DMA((2, 2, 4)), DMA((2, 2, 4)), DMA((2, 8)), DMA((2, 8)), DMA((3,)), DMA((3,)),
            DMA((2, 2)), DMA((2, 2)), DMA((2, 7, 4)), DMA((2, 7, 4)), DMA((NH,)), DMA((NH,)),
            DMA((2, NH)), DMA((2, NH)),
            DMA((7, 8)), DMA((7, 8)), DMA((2, 2)), DMA((2, 2)), DMA((NH,)), DMA((NH,)), DMA((NC,)), DMA((NC,)),
        ],
        compiler_params=pltpu.CompilerParams(collective_id=1, has_side_effects=True, vmem_limit_bytes=60 << 20),
        name="layer",
    )(*args)


def hand_on(*args):
    parts = [(n, None) for n in range(5)] + [(n, e) for n in range(5, 8) for e in range(2)]

    def kernel(*refs):
        into, sems = refs[16:24], refs[24]

        def at(ref, e):
            return ref if e is None else ref.at[e]

        ins = [pltpu.make_async_copy(at(refs[n], e), at(into[n], e), sems.at[0, k]) for k, (n, e) in enumerate(parts)]
        outs = [pltpu.make_async_copy(at(into[n], e), at(refs[n + 8], e), sems.at[1, k]) for k, (n, e) in enumerate(parts)]
        for c in ins:
            c.start()
        for a, b in zip(ins, outs):
            a.wait()
            b.start()
        for c in outs:
            c.wait()

    return pl.pallas_call(
        kernel,
        out_shape=tuple(SDS(s, t) for s, t in RESULTS),
        in_specs=[ANY] * 8,
        out_specs=(ANY,) * 8,
        scratch_shapes=[pltpu.VMEM(s, t) for s, t in RESULTS] + [DMA((2, 11))],
        compiler_params=pltpu.CompilerParams(vmem_limit_bytes=60 << 20),
        name="hand_on",
    )(*args)


def per_device(queries, key_rows, value_rows, output_weight, residual_stream, norm_gain, expert_ids,
               combine_weights, gate_weight, up_weight, down_weight, cotangent):
    results = call_layer(
        queries, key_rows, value_rows, output_weight, residual_stream, norm_gain.reshape(1, W), expert_ids.T,
        combine_weights.T, gate_weight, up_weight, down_weight, cotangent)
    moe, attg, resg, gaing, combg, dgate, dup, ddown = hand_on(*results)
    return moe, attg, resg, gaing.reshape(W), combg.T, dgate, dup, ddown


def solution(mesh):
    return jax.shard_map(
        per_device,
        mesh=mesh,
        in_specs=(
            P("ctx", "head"), P("ctx", "head"), P("ctx", "head"), P("head", None), P("ctx", "head"), P("head"),
            P("ctx", None), P("ctx", None), P("ctx", "head", None), P("ctx", "head", None),
            P("ctx", "head", None), P("ctx", "head"),
        ),
        out_specs=(
            P("ctx", "head"), P("ctx", "head"), P("ctx", "head"), P("head"), P("ctx", None),
            P("ctx", "head", None), P("ctx", "head", None), P("ctx", "head", None),
        ),
        check_vma=False,
    )
```

```python
import jax
import jax.numpy as jnp
from jax import lax
from jax.experimental import pallas as pl
from jax.experimental.pallas import tpu as pltpu
from jax.sharding import PartitionSpec as P

D = 2048
TOP = 6
DH = 128
NC = 32
NH = 8
TOK = 128
W = 256
FD = 176
PART = 256
PARTS = 2
CAP = 16
ROWS = NC * CAP
SLOTS = 2 * ROWS
MESH = pl.DeviceIdType.MESH
BF = jnp.bfloat16
F32 = jnp.float32


def dot(a, b, ca=1, cb=0):
    return lax.dot_general(a, b, (((ca,), (cb,)), ((), ())), preferred_element_type=F32)


def coords():
    return lax.axis_index("ctx"), lax.axis_index("head")


def head_of(xl, y):
    return xl * 4 + lax.rem(y + 4, 4)


def ctx_of(xh, z, core):
    return xh * 16 + lax.rem(z + 8, 8) * 2 + core


def remote(src, dst, ssem, rsem, ctx, head):
    return pltpu.make_async_remote_copy(
        src, dst, ssem, rsem, device_id=(ctx, head), device_id_type=MESH
    )


def greet(bar):
    i, h = coords()

    def ctx_peer(o, c):
        pl.semaphore_signal(bar, 1, device_id=(lax.rem(i + o, NC), h), device_id_type=MESH)
        return c

    def head_peer(o, c):
        pl.semaphore_signal(bar, 1, device_id=(i, lax.rem(h + o, NH)), device_id_type=MESH)
        return c

    lax.fori_loop(1, NC, ctx_peer, 0)
    lax.fori_loop(1, NH, head_peer, 0)


def routing(ids, cw):
    eio = lax.broadcasted_iota(jnp.int32, (TOK, 2 * NC), 1)
    hot = jnp.zeros((TOK, 2 * NC), F32)
    wts = jnp.zeros((TOK, 2 * NC), F32)
    for k in range(TOP):
        m = ids[:, k : k + 1] == eio
        hot = hot + jnp.where(m, 1.0, 0.0)
        wts = wts + jnp.where(m, cw[:, k : k + 1], 0.0)
    r = lax.broadcasted_iota(jnp.int32, (TOK, TOK), 0)
    c = lax.broadcasted_iota(jnp.int32, (TOK, TOK), 1)
    lower = jnp.where(c < r, 1.0, 0.0).astype(BF)
    earlier = dot(lower, hot.astype(BF))
    n = lax.broadcasted_iota(jnp.int32, (2 * NC, SLOTS), 1)
    e = lax.broadcasted_iota(jnp.int32, (2 * NC, SLOTS), 0)
    spread = jnp.where(e == 2 * (lax.rem(n, ROWS) // CAP) + n // ROWS, 1.0, 0.0).astype(BF)
    hot_n = dot(hot.astype(BF), spread)
    earlier_n = dot(earlier.astype(BF), spread)
    slot = lax.rem(lax.broadcasted_iota(jnp.int32, (TOK, SLOTS), 1), CAP).astype(F32)
    place = jnp.where((hot_n > 0.5) & (earlier_n == slot), 1.0, 0.0)
    hi = wts.astype(BF)
    lo = (wts - hi.astype(F32)).astype(BF)
    whi = place * dot(hi, spread)
    wlo = place * dot(lo, spread)
    return place.astype(BF), whi.astype(BF), wlo.astype(BF)


def start_dispatch(packed, g, asend, arecv, lsem, e):
    i, h = coords()
    mine = pl.ds(pl.multiple_of(i * CAP, CAP), CAP)

    def send(o, c):
        d = lax.rem(i + o, NC)
        theirs = pl.ds(pl.multiple_of(d * CAP, CAP), CAP)
        remote(packed.at[e, theirs], g.at[h, e, mine], asend.at[e], arecv.at[e], d, h).start()
        return c

    lax.fori_loop(1, NC, send, 0)
    own = pltpu.make_async_copy(packed.at[e, mine], g.at[h, e, mine], lsem)
    own.start()
    own.wait()


def dispatched(packed, g, asend, arecv, e):
    i, h = coords()
    most = pl.ds(0, (NC - 1) * CAP)
    return remote(packed.at[e, most], g.at[h, e, most], asend.at[e], arecv.at[e], i, 7 - h)


class HeadGather:
    parts = [(e, q) for e in range(2) for q in range(PARTS)]

    def __init__(self, g, ssem, rsem):
        i, h = coords()
        xl, y = h // 4, lax.rem(h, 4)
        self.g, self.ssem, self.rsem, self.i, self.h = g, ssem, rsem, i, h
        self.xp, self.up, self.down = head_of(1 - xl, y), head_of(xl, y + 1), head_of(xl, y - 1)
        self.pup, self.pdown = head_of(1 - xl, y + 1), head_of(1 - xl, y - 1)
        self.far, self.pfar = head_of(xl, y + 2), head_of(1 - xl, y + 2)

    def copy(self, kind, n, block, target):
        e, q = self.parts[n]
        view = self.g.at[block, e, pl.ds(q * PART, PART)]
        return remote(view, view, self.ssem.at[kind, n], self.rsem.at[kind, n], self.i, target)

    def own(self, n):
        self.copy(0, n, self.h, self.xp).start()
        self.copy(1, n, self.h, self.up).start()
        self.copy(2, n, self.h, self.down).start()

    def pass_on(self, n):
        self.copy(0, n, self.xp, self.xp).wait_recv()
        self.copy(3, n, self.xp, self.up).start()
        self.copy(4, n, self.xp, self.down).start()
        if n % 2 == 0:
            self.copy(1, n, self.down, self.up).wait_recv()
            self.copy(5, n, self.down, self.up).start()
        else:
            self.copy(2, n, self.up, self.down).wait_recv()
            self.copy(5, n, self.up, self.down).start()

    def far_on(self, n):
        self.copy(5, n, self.far, self.up).wait_recv()
        self.copy(6, n, self.far, self.xp).start()

    def whole(self, n):
        if n % 2 == 0:
            self.copy(2, n, self.up, self.up).wait_recv()
        else:
            self.copy(1, n, self.down, self.up).wait_recv()
        self.copy(3, n, self.pdown, self.up).wait_recv()
        self.copy(4, n, self.pup, self.up).wait_recv()
        self.copy(6, n, self.pfar, self.up).wait_recv()

    def drain(self):
        for n in range(len(self.parts)):
            self.copy(0, n, self.h, self.xp).wait_send()
            self.copy(1, n, self.h, self.up).wait_send()
            self.copy(2, n, self.h, self.down).wait_send()
            self.copy(3, n, self.xp, self.up).wait_send()
            self.copy(4, n, self.xp, self.down).wait_send()
            self.copy(5, n, self.down, self.up).wait_send()
            self.copy(6, n, self.far, self.xp).wait_send()


def key_flow(kv, zs, zr, ks, kr):
    i, h = coords()
    xh, z, core = i // 16, lax.rem(i // 2, 8), lax.rem(i, 2)
    up, down = ctx_of(xh, z + 1, core), ctx_of(xh, z - 1, core)
    twin = ctx_of(xh, z, 1 - core)
    lanes = [(k, d) for k in range(2) for d in range(2)]

    def hops(k, d):
        return 4 if k == d else 3

    def view(k, dz, c):
        return kv.at[lax.rem(z + dz + 8, 8) * 2 + c, k]

    def ring(k, d, s):
        v = view(k, -s if d == 0 else s, core)
        return remote(v, v, zs.at[k, d, s], zr.at[k, d, s], up if d == 0 else down, h)

    def landed(k, d, s):
        v = view(k, -s - 1 if d == 0 else s + 1, core)
        return remote(v, v, zs.at[k, d, s], zr.at[k, d, s], up if d == 0 else down, h)

    def share(k, dz, c):
        v = view(k, dz, c)
        return remote(v, v, ks.at[k, dz % 8], kr.at[k, dz % 8], twin, h)

    for k, d in lanes:
        ring(k, d, 0).start()
    for k in range(2):
        share(k, 0, core).start()
    yield
    for s in range(4):
        for k, d in lanes:
            if s < hops(k, d):
                landed(k, d, s).wait_recv()
                if s + 1 < hops(k, d):
                    ring(k, d, s + 1).start()
                share(k, -s - 1 if d == 0 else s + 1, core).start()
        yield
    for k in range(2):
        for dz in range(-4, 4):
            share(k, dz, 1 - core).wait_recv()
    yield
    for k, d in lanes:
        for s in range(hops(k, d)):
            ring(k, d, s).wait_send()
    for k in range(2):
        for dz in range(-4, 4):
            share(k, dz, core).wait_send()
    yield


def to_rows(columns):
    lane = lax.broadcasted_iota(jnp.int32, (TOK, TOK), 1)
    packed = jnp.zeros((TOK, TOK), F32)
    for k, c in enumerate(columns):
        packed = jnp.where(lane == k, c, packed)
    return packed.T[0:8]


def to_columns(rows):
    return jnp.concatenate([rows, jnp.zeros((TOK - 8, TOK), F32)], axis=0).T


def layer_kernel(q_in, k_in, v_in, w_in, res_in, gain, ids_in, cw_in, wg_in, wu_in, wd_in, cot_in,
                 moe_out, attg_out, resg_out, gaing_out, combg_out, dgate_out, dup_out, ddown_out,
                 qb, kv, w_ref, res, ids_ref, cw_ref, wg, wu, wd, cot_ref,
                 place, whi, wlo, packed, gcot, gin, ob, os, terms, got, stats, stats2, normed, inv,
                 act_s, gd_s, ud_s, gp_s, up_s, t_ref, r_ref, fin, picked, rgb, gsum,
                 moe, attg, resg, gaing, combg, dgate, dup, ddown,
                 lsem, osem, zs, zr, ks, kr, xs, xr, asend, arecv, gs, gr, ts, tr, ss, sr,
                 fs, fr, bs, br, rs, rr, qs, qr):
    i, h = coords()
    xh, z, core = i // 16, lax.rem(i // 2, 8), lax.rem(i, 2)
    xl, y = h // 4, lax.rem(h, 4)
    xp, up, down = head_of(1 - xl, y), head_of(xl, y + 1), head_of(xl, y - 1)
    pup, pdown = head_of(1 - xl, y + 1), head_of(1 - xl, y - 1)
    far, pfar = head_of(xl, y + 2), head_of(1 - xl, y + 2)
    other = ctx_of(1 - xh, z, core)
    HR = ROWS // 2
    seat = lax.rem(i, 16)

    loads = [
        pltpu.make_async_copy(s, d, lsem.at[n])
        for n, (s, d) in enumerate((
            (k_in, kv.at[seat, 0]), (v_in, kv.at[seat, 1]), (q_in, qb.at[0]), (ids_in, ids_ref), (cw_in, cw_ref),
            (cot_in, cot_ref), (w_in, w_ref), (res_in, res), (wg_in, wg), (wu_in, wu), (wd_in, wd),
        ))
    ]
    for c in loads:
        c.start()
    bar = pltpu.get_barrier_semaphore()
    greet(bar)
    for c in loads[3:6]:
        c.wait()
    pad = jnp.zeros((TOK - TOP, TOK), F32)
    ids = jnp.concatenate([ids_ref[...].astype(F32), pad], axis=0).T.astype(jnp.int32)
    cw = jnp.concatenate([cw_ref[...], pad], axis=0).T
    p, hi, lo = routing(ids, cw)
    place[...] = p
    whi[...] = hi
    wlo[...] = lo
    cot = cot_ref[...]
    rows = dot(hi, cot, 0, 0) + dot(lo, cot, 0, 0)
    packed[0] = rows.astype(BF).reshape(2, ROWS, W)
    for c in loads[0:3]:
        c.wait()
    pl.semaphore_wait(bar, NC - 1 + NH - 1)

    def sent(part, g, e):
        return dispatched(packed.at[part], g, asend.at[part], arecv.at[part], e)

    keys = key_flow(kv, zs, zr, ks, kr)
    next(keys)
    q_swap = remote(qb.at[0], qb.at[1], xs.at[0], xr.at[0], other, h)
    q_swap.start()
    cots = HeadGather(gcot, gs.at[0], gr.at[0])
    next(keys)
    next(keys)
    next(keys)
    start_dispatch(packed.at[0], gcot, asend.at[0], arecv.at[0], lsem.at[11], 0)
    next(keys)
    start_dispatch(packed.at[0], gcot, asend.at[0], arecv.at[0], lsem.at[11], 1)
    next(keys)

    q_swap.wait_recv()
    q2 = jnp.concatenate([qb[0], qb[1]], axis=0)
    r = lax.broadcasted_iota(jnp.int32, (2 * TOK, 1), 0)
    limit = jnp.where(r < TOK, seat * TOK + r, jnp.where(xh == 0, 16 * TOK - 1, -1))
    allowed = lax.broadcasted_iota(jnp.int32, (2 * TOK, 16 * TOK), 1) <= limit
    outs, tops, sums = [], [], []
    for n in range(2):
        cs = slice(n * DH, (n + 1) * DH)
        s = dot(q2[:, cs], kv[:, 0, :, cs].reshape(16 * TOK, DH), 1, 1) * DH ** (-0.5)
        s = jnp.where(allowed, s, -1e30)
        m = jnp.max(s, axis=1, keepdims=True)
        wts = jnp.exp(s - m)
        tot = jnp.sum(wts, axis=1, keepdims=True)
        o = dot(wts.astype(BF), kv[:, 1, :, cs].reshape(16 * TOK, DH)) / tot
        outs.append(o)
        tops.append(m)
        sums.append(tot)
    seen = jnp.where(xh == 0, 1.0, 0.0)
    ob[0] = jnp.concatenate([o[TOK:] for o in outs], axis=1).astype(BF)
    os[0] = to_rows([tops[0][TOK:], sums[0][TOK:] * seen, tops[1][TOK:], sums[1][TOK:] * seen])
    o_swap = remote(ob.at[0], ob.at[1], xs.at[1], xr.at[1], other, h)
    s_swap = remote(os.at[0], os.at[1], xs.at[2], xr.at[2], other, h)
    o_swap.start()
    s_swap.start()
    sent(0, gcot, 0).wait_recv()
    cots.own(0)
    cots.own(1)
    loads[6].wait()
    loads[7].wait()
    s_swap.wait_recv()
    o_swap.wait_recv()
    there = to_columns(os[1])
    att = []
    for n in range(2):
        m1, l1 = tops[n][:TOK], sums[n][:TOK]
        m2, l2 = there[:, 2 * n : 2 * n + 1], there[:, 2 * n + 1 : 2 * n + 2]
        m = jnp.maximum(m1, m2)
        a1, a2 = l1 * jnp.exp(m1 - m), l2 * jnp.exp(m2 - m)
        o2 = ob[1, :, n * DH : (n + 1) * DH].astype(F32)
        att.append((a1 * outs[n][:TOK] + a2 * o2) / (a1 + a2))
    att = jnp.concatenate(att, axis=1).astype(BF)

    t = dot(att, w_ref[...]).astype(BF)
    for d in range(NH):
        terms[d] = t[:, d * W : (d + 1) * W]
    for o in range(1, NH):
        d = lax.rem(h + o, NH)
        remote(terms.at[d], got.at[o], ts.at[o], tr.at[o], i, d).start()

    cots.pass_on(0)
    hidden = res[...].astype(F32) + terms[h].astype(F32)
    for o in range(1, NH):
        d = lax.rem(h + o, NH)
        remote(terms.at[d], got.at[o], ts.at[o], tr.at[o], i, d).wait()
        hidden = hidden + got[o].astype(F32)
    stats[0] = to_rows([jnp.sum(hidden * hidden, axis=1, keepdims=True)])
    for o in range(1, NH):
        remote(stats.at[0], stats.at[o], ss.at[0, o], sr.at[0, o], i, lax.rem(h + o, NH)).start()
    sent(0, gcot, 1).wait_recv()
    cots.own(2)
    cots.own(3)
    cots.pass_on(1)
    cots.far_on(0)
    total = stats[0]
    for o in range(1, NH):
        remote(stats.at[0], stats.at[o], ss.at[0, o], sr.at[0, o], i, lax.rem(h + o, NH)).wait()
        total = total + stats[o]
    inverse = lax.rsqrt(to_columns(total)[:, 0:1] / D + 1e-06)
    inv[...] = jnp.broadcast_to(inverse, (TOK, TOK))
    nrm = hidden * inverse
    normed[...] = nrm
    inputs = (nrm * gain[...]).astype(BF)
    packed[1] = dot(place[...], inputs, 0, 0).astype(BF).reshape(2, ROWS, W)
    start_dispatch(packed.at[1], gin, asend.at[1], arecv.at[1], lsem.at[11], 0)
    start_dispatch(packed.at[1], gin, asend.at[1], arecv.at[1], lsem.at[11], 1)
    cots.pass_on(2)
    cots.far_on(1)
    cots.pass_on(3)
    cots.far_on(2)
    cots.far_on(3)
    for c in loads[8:]:
        c.wait()

    def rows_of(ref, e, lo, n):
        return jnp.concatenate([ref[b, e, lo : lo + n] for b in range(NH)], axis=1)

    def forward(e, hf):
        sl = slice(hf * HR, (hf + 1) * HR)
        x = rows_of(gin, e, hf * HR, HR)
        gp = dot(x, wg[e], 1, 1)
        u = dot(x, wu[e], 1, 1)
        gp_s[e, sl] = gp
        up_s[e, sl] = u
        act = (gp * jax.nn.sigmoid(gp) * u).astype(BF)
        act_s[e, sl] = act
        for b in range(NH):
            t_ref[0, b, e, sl] = dot(act, wd[e, :, b * W : (b + 1) * W]).astype(BF)

    def backward(e, hf):
        sl = slice(hf * HR, (hf + 1) * HR)
        x = rows_of(gcot, e, hf * HR, HR)
        ag = dot(x, wd[e], 1, 1)
        gp = gp_s[e, sl]
        s = jax.nn.sigmoid(gp)
        gd = (ag * up_s[e, sl] * s * (1.0 + gp * (1.0 - s))).astype(BF)
        ud = (ag * gp * s).astype(BF)
        gd_s[e, sl] = gd
        ud_s[e, sl] = ud
        for b in range(NH):
            cs = slice(b * W, (b + 1) * W)
            t_ref[1, b, e, sl] = (dot(gd, wg[e, :, cs]) + dot(ud, wu[e, :, cs])).astype(BF)

    def weight_grads(e):
        for b in range(NH):
            cs = slice(b * W, (b + 1) * W)
            x = gin[b, e]
            dgate[e, :, cs] = dot(gd_s[e], x, 0, 0).astype(BF)
            dup[e, :, cs] = dot(ud_s[e], x, 0, 0).astype(BF)
            ddown[e, :, cs] = dot(act_s[e], gcot[b, e], 0, 0).astype(BF)

    def tview(f, block):
        t, e, q = f
        return t_ref.at[t, block, e, pl.ds(q * PART, PART)]

    def index(f):
        return (f[0] * 2 + f[1]) * PARTS + f[2]

    def copy(kind, f, block, target):
        n = index(f)
        return remote(tview(f, block), r_ref.at[n, kind], fs.at[kind, n], fr.at[kind, n], i, target)

    def add(f, block, kinds):
        acc = tview(f, block)[...].astype(F32)
        for kind in kinds:
            acc = acc + r_ref[index(f), kind].astype(F32)
        return acc.astype(BF)

    def stage0(f):
        copy(0, f, pfar, xp).start()
        copy(1, f, pup, up).start()
        copy(2, f, pdown, down).start()
        if f[2] % 2 == 0:
            copy(6, f, down, down).start()
        else:
            copy(5, f, up, up).start()

    def stage1(f):
        copy(0, f, far, xp).wait_recv()
        tview(f, far)[...] = add(f, far, (0,))
        copy(3, f, far, up if f[2] % 2 == 0 else down).start()
        copy(1, f, xp, up).wait_recv()
        copy(2, f, xp, up).wait_recv()
        tview(f, xp)[...] = add(f, xp, (1, 2))
        copy(4, f, xp, xp).start()

    def stage2(f):
        block = up if f[2] % 2 == 0 else down
        copy(3, f, block, up).wait_recv()
        tview(f, block)[...] = add(f, block, (3,))
        copy(5 if f[2] % 2 == 0 else 6, f, block, block).start()

    def stage3(f):
        t, e, q = f
        for kind in (4, 5, 6):
            copy(kind, f, h, up).wait_recv()
        fin[t, e, q * PART : (q + 1) * PART] = add(f, h, (4, 5, 6))

        def send(k, c):
            d = q * (PART // CAP) + k

            @pl.when(d != i)
            def _():
                back(t, e, d).start()

            return c

        lax.fori_loop(0, PART // CAP, send, 0)

    def back(t, e, d):
        return remote(fin.at[t, e, pl.ds(pl.multiple_of(d * CAP, CAP), CAP)], picked.at[t, e, i],
                      bs.at[t, e], br.at[t, e], d, h)

    def drain(f):
        for kind, block in ((0, pfar), (1, pup), (2, pdown), (3, far), (4, xp), (5, up), (6, down)):
            copy(kind, f, block, xp).wait_send()

    flows = [(t, e, q) for t in range(2) for e in range(2) for q in range(PARTS)]
    count = len(flows)
    outward = [
        pltpu.make_async_copy(s, d, osem.at[n])
        for n, (s, d) in enumerate((
            (moe, moe_out), (attg, attg_out), (resg, resg_out), (gaing, gaing_out), (combg, combg_out),
            (dgate, dgate_out), (dup, dup_out), (ddown, ddown_out),
        ))
    ]

    def landed(t):
        mine = pl.ds(pl.multiple_of(i * CAP, CAP), CAP)
        for e in range(2):
            own = pltpu.make_async_copy(fin.at[t, e, mine], picked.at[t, e, i], lsem.at[11])
            own.start()
            own.wait()
            part = picked.at[t, e, pl.ds(0, NC - 1)]
            remote(part, part, bs.at[t, e], br.at[t, e], i, xp).wait()
        return picked[t].reshape(SLOTS, W)

    def combine():
        rows = landed(0)
        moe[...] = (dot(whi[...], rows) + dot(wlo[...], rows)).astype(BF)
        outward[0].start()
        every = dot(cot_ref[...], rows, 1, 1) * place[...].astype(F32)
        n = lax.broadcasted_iota(jnp.int32, (TOK, SLOTS), 1)
        expert = 2 * (lax.rem(n, ROWS) // CAP) + n // ROWS
        columns = [
            jnp.sum(jnp.where(expert == ids[:, k : k + 1], every, 0.0), axis=1, keepdims=True) for k in range(TOP)
        ]
        return columns

    columns = []

    def tick(n):
        if n < count:
            t, e, q = flows[n]
            (forward if t == 0 else backward)(e, q)
            stage0(flows[n])
        if 0 <= n - 1 < count:
            stage1(flows[n - 1])
        if 0 <= n - 2 < count:
            stage2(flows[n - 2])
        if 0 <= n - 3 < count:
            stage3(flows[n - 3])
        if n == 3 * PARTS:
            weight_grads(0)
        if n == 3 * PARTS + 2:
            columns.extend(combine())

    ins = HeadGather(gin, gs.at[1], gr.at[1])
    sent(1, gin, 0).wait_recv()
    ins.own(0)
    ins.own(1)
    ins.pass_on(0)
    sent(1, gin, 1).wait_recv()
    ins.own(2)
    ins.pass_on(1)
    ins.far_on(0)
    ins.own(3)
    ins.pass_on(2)
    ins.far_on(1)
    ins.whole(0)
    tick(0)
    ins.pass_on(3)
    ins.far_on(2)
    ins.whole(1)
    tick(1)
    ins.far_on(3)
    ins.whole(2)
    tick(2)
    ins.whole(3)
    tick(3)
    for n in range(4):
        cots.whole(n)
    for n in range(2 * PARTS, count + 3):
        tick(n)

    rows = landed(1)
    input_grad = dot(place[...], rows)
    nrm = normed[...]
    gsum[0] = jnp.broadcast_to(jnp.sum(input_grad * nrm, axis=0, keepdims=True), (8, W))

    def gain_copy(o):
        d = lax.rem(i + o, NC)
        return remote(gsum.at[0], gsum.at[o], qs.at[o], qr.at[o], d, h)

    def gain_start(o, c):
        gain_copy(o).start()
        return c

    ng = input_grad * gain[...]
    stats2[0] = to_rows(columns + [jnp.sum(ng * nrm, axis=1, keepdims=True)])
    for o in range(1, NH):
        remote(stats2.at[0], stats2.at[o], ss.at[1, o], sr.at[1, o], i, lax.rem(h + o, NH)).start()
    lax.fori_loop(1, NC, gain_start, 0)
    total = stats2[0]
    for o in range(1, NH):
        remote(stats2.at[0], stats2.at[o], ss.at[1, o], sr.at[1, o], i, lax.rem(h + o, NH)).wait()
        total = total + stats2[o]
    combg[...] = total[0:TOP]
    outward[4].start()
    centre = to_columns(total)[:, TOP : TOP + 1] / D
    rg = (inv[:, 0:1] * (ng - nrm * centre)).astype(BF)
    resg[...] = rg
    outward[2].start()
    rgb[h] = rg
    for o in range(1, NH):
        d = lax.rem(h + o, NH)
        remote(rgb.at[h], rgb.at[h], rs.at[o], rr.at[o], i, d).start()

    weight_grads(1)
    for c in outward[5:]:
        c.start()

    def gain_wait(o, c):
        gain_copy(o).wait()
        return c + gsum[o]

    gaing[...] = lax.fori_loop(1, NC, gain_wait, gsum[0])[0:1]
    outward[3].start()
    for f in flows:
        drain(f)
    for part in range(2):
        for e in range(2):
            sent(part, (gcot, gin)[part], e).wait_send()
    cots.drain()
    ins.drain()
    q_swap.wait_send()
    o_swap.wait_send()
    s_swap.wait_send()
    for _ in keys:
        pass
    for o in range(1, NH):
        s = lax.rem(h - o + NH, NH)
        remote(rgb.at[s], rgb.at[s], rs.at[o], rr.at[o], i, s).wait()
    whole = jnp.concatenate([rgb[b] for b in range(NH)], axis=1)
    attg[...] = dot(whole, w_ref[...], 1, 1).astype(BF)
    outward[1].start()
    for c in outward:
        c.wait()


VM = pl.BlockSpec(memory_space=pltpu.VMEM)
ANY = pl.BlockSpec(memory_space=pl.ANY)
DMA = pltpu.SemaphoreType.DMA
SDS = jax.ShapeDtypeStruct
RESULTS = (
    ((TOK, W), BF), ((TOK, W), BF), ((TOK, W), BF), ((1, W), F32), ((TOP, TOK), F32),
    ((2, FD, D), BF), ((2, FD, D), BF), ((2, FD, D), BF),
)


def call_layer(*args):
    v = pltpu.VMEM
    return pl.pallas_call(
        layer_kernel,
        out_shape=tuple(SDS(s, t) for s, t in RESULTS),
        in_specs=[ANY] * 5 + [VM] + [ANY] * 6,
        out_specs=(ANY,) * 8,
        scratch_shapes=[
            v((2, TOK, W), BF), v((16, 2, TOK, W), BF), v((W, D), BF), v((TOK, W), BF),
            v((TOP, TOK), jnp.int32), v((TOP, TOK), F32),
            v((2, FD, D), BF), v((2, FD, D), BF), v((2, FD, D), BF), v((TOK, W), BF),
            v((TOK, SLOTS), BF), v((TOK, SLOTS), BF), v((TOK, SLOTS), BF),
            v((2, 2, ROWS, W), BF), v((NH, 2, ROWS, W), BF), v((NH, 2, ROWS, W), BF),
            v((2, TOK, W), BF), v((2, 8, TOK), F32), v((NH, TOK, W), BF), v((NH, TOK, W), BF),
            v((NH, 8, TOK), F32), v((NH, 8, TOK), F32), v((TOK, W), F32), v((TOK, TOK), F32),
            v((2, ROWS, FD), BF), v((2, ROWS, FD), BF), v((2, ROWS, FD), BF),
            v((2, ROWS, FD), F32), v((2, ROWS, FD), F32),
            v((2, NH, 2, ROWS, W), BF), v((4 * PARTS, 7, PART, W), BF), v((2, 2, ROWS, W), BF),
            v((2, 2, NC, CAP, W), BF), v((NH, TOK, W), BF), v((NC, 8, W), F32),
            *[v(s, t) for s, t in RESULTS],
            DMA((12,)), DMA((8,)),
            DMA((2, 2, 4)), DMA((2, 2, 4)), DMA((2, 8)), DMA((2, 8)), DMA((3,)), DMA((3,)),
            DMA((2, 2)), DMA((2, 2)), DMA((2, 7, 2 * PARTS)), DMA((2, 7, 2 * PARTS)), DMA((NH,)), DMA((NH,)),
            DMA((2, NH)), DMA((2, NH)),
            DMA((7, 4 * PARTS)), DMA((7, 4 * PARTS)), DMA((2, 2)), DMA((2, 2)), DMA((NH,)), DMA((NH,)), DMA((NC,)), DMA((NC,)),
        ],
        compiler_params=pltpu.CompilerParams(collective_id=1, has_side_effects=True, vmem_limit_bytes=60 << 20),
        name="layer",
    )(*args)


def hand_on(*args):
    parts = [(n, None) for n in range(5)] + [(n, e) for n in range(5, 8) for e in range(2)]

    def kernel(*refs):
        into, sems = refs[16:24], refs[24]

        def at(ref, e):
            return ref if e is None else ref.at[e]

        ins = [pltpu.make_async_copy(at(refs[n], e), at(into[n], e), sems.at[0, k]) for k, (n, e) in enumerate(parts)]
        outs = [pltpu.make_async_copy(at(into[n], e), at(refs[n + 8], e), sems.at[1, k]) for k, (n, e) in enumerate(parts)]
        for c in ins:
            c.start()
        for a, b in zip(ins, outs):
            a.wait()
            b.start()
        for c in outs:
            c.wait()

    return pl.pallas_call(
        kernel,
        out_shape=tuple(SDS(s, t) for s, t in RESULTS),
        in_specs=[ANY] * 8,
        out_specs=(ANY,) * 8,
        scratch_shapes=[pltpu.VMEM(s, t) for s, t in RESULTS] + [DMA((2, 11))],
        compiler_params=pltpu.CompilerParams(vmem_limit_bytes=60 << 20),
        name="hand_on",
    )(*args)


def per_device(queries, key_rows, value_rows, output_weight, residual_stream, norm_gain, expert_ids,
               combine_weights, gate_weight, up_weight, down_weight, cotangent):
    results = call_layer(
        queries, key_rows, value_rows, output_weight, residual_stream, norm_gain.reshape(1, W), expert_ids.T,
        combine_weights.T, gate_weight, up_weight, down_weight, cotangent)
    moe, attg, resg, gaing, combg, dgate, dup, ddown = hand_on(*results)
    return moe, attg, resg, gaing.reshape(W), combg.T, dgate, dup, ddown


def solution(mesh):
    return jax.shard_map(
        per_device,
        mesh=mesh,
        in_specs=(
            P("ctx", "head"), P("ctx", "head"), P("ctx", "head"), P("head", None), P("ctx", "head"), P("head"),
            P("ctx", None), P("ctx", None), P("ctx", "head", None), P("ctx", "head", None),
            P("ctx", "head", None), P("ctx", "head"),
        ),
        out_specs=(
            P("ctx", "head"), P("ctx", "head"), P("ctx", "head"), P("head"), P("ctx", None),
            P("ctx", "head", None), P("ctx", "head", None), P("ctx", "head", None),
        ),
        check_vma=False,
    )
```

```python
import jax
import jax.numpy as jnp
from jax import lax
from jax.experimental import pallas as pl
from jax.experimental.pallas import tpu as pltpu
from jax.sharding import PartitionSpec as P

D = 2048
TOP = 6
DH = 128
NC = 32
NH = 8
TOK = 128
W = 256
FD = 176
PART = 256
PARTS = 2
CAP = 16
ROWS = NC * CAP
SLOTS = 2 * ROWS
MESH = pl.DeviceIdType.MESH
BF = jnp.bfloat16
F32 = jnp.float32


def dot(a, b, ca=1, cb=0):
    return lax.dot_general(a, b, (((ca,), (cb,)), ((), ())), preferred_element_type=F32)


def coords():
    return lax.axis_index("ctx"), lax.axis_index("head")


def head_of(xl, y):
    return xl * 4 + lax.rem(y + 4, 4)


def ctx_of(xh, z, core):
    return xh * 16 + lax.rem(z + 8, 8) * 2 + core


def remote(src, dst, ssem, rsem, ctx, head):
    return pltpu.make_async_remote_copy(
        src, dst, ssem, rsem, device_id=(ctx, head), device_id_type=MESH
    )


def greet(bar):
    i, h = coords()

    def ctx_peer(o, c):
        pl.semaphore_signal(bar, 1, device_id=(lax.rem(i + o, NC), h), device_id_type=MESH)
        return c

    def head_peer(o, c):
        pl.semaphore_signal(bar, 1, device_id=(i, lax.rem(h + o, NH)), device_id_type=MESH)
        return c

    lax.fori_loop(1, NC, ctx_peer, 0)
    lax.fori_loop(1, NH, head_peer, 0)


def routing(ids, cw):
    eio = lax.broadcasted_iota(jnp.int32, (TOK, 2 * NC), 1)
    hot = jnp.zeros((TOK, 2 * NC), F32)
    wts = jnp.zeros((TOK, 2 * NC), F32)
    for k in range(TOP):
        m = ids[:, k : k + 1] == eio
        hot = hot + jnp.where(m, 1.0, 0.0)
        wts = wts + jnp.where(m, cw[:, k : k + 1], 0.0)
    r = lax.broadcasted_iota(jnp.int32, (TOK, TOK), 0)
    c = lax.broadcasted_iota(jnp.int32, (TOK, TOK), 1)
    lower = jnp.where(c < r, 1.0, 0.0).astype(BF)
    earlier = dot(lower, hot.astype(BF))
    n = lax.broadcasted_iota(jnp.int32, (2 * NC, SLOTS), 1)
    e = lax.broadcasted_iota(jnp.int32, (2 * NC, SLOTS), 0)
    spread = jnp.where(e == 2 * (lax.rem(n, ROWS) // CAP) + n // ROWS, 1.0, 0.0).astype(BF)
    hot_n = dot(hot.astype(BF), spread)
    earlier_n = dot(earlier.astype(BF), spread)
    slot = lax.rem(lax.broadcasted_iota(jnp.int32, (TOK, SLOTS), 1), CAP).astype(F32)
    place = jnp.where((hot_n > 0.5) & (earlier_n == slot), 1.0, 0.0)
    hi = wts.astype(BF)
    lo = (wts - hi.astype(F32)).astype(BF)
    whi = place * dot(hi, spread)
    wlo = place * dot(lo, spread)
    return place.astype(BF), whi.astype(BF), wlo.astype(BF)


def start_dispatch(packed, g, asend, arecv, lsem, e):
    i, h = coords()
    mine = pl.ds(pl.multiple_of(i * CAP, CAP), CAP)

    def send(o, c):
        d = lax.rem(i + o, NC)
        theirs = pl.ds(pl.multiple_of(d * CAP, CAP), CAP)
        remote(packed.at[e, theirs], g.at[h, e, mine], asend.at[e], arecv.at[e], d, h).start()
        return c

    lax.fori_loop(1, NC, send, 0)
    own = pltpu.make_async_copy(packed.at[e, mine], g.at[h, e, mine], lsem)
    own.start()
    own.wait()


def dispatched(packed, g, asend, arecv, e):
    i, h = coords()
    most = pl.ds(0, (NC - 1) * CAP)
    return remote(packed.at[e, most], g.at[h, e, most], asend.at[e], arecv.at[e], i, 7 - h)


class HeadGather:
    parts = [(e, q) for e in range(2) for q in range(PARTS)]

    def __init__(self, g, ssem, rsem):
        i, h = coords()
        xl, y = h // 4, lax.rem(h, 4)
        self.g, self.ssem, self.rsem, self.i, self.h = g, ssem, rsem, i, h
        self.xp, self.up, self.down = head_of(1 - xl, y), head_of(xl, y + 1), head_of(xl, y - 1)
        self.pup, self.pdown = head_of(1 - xl, y + 1), head_of(1 - xl, y - 1)
        self.far, self.pfar = head_of(xl, y + 2), head_of(1 - xl, y + 2)

    def copy(self, kind, n, block, target):
        e, q = self.parts[n]
        view = self.g.at[block, e, pl.ds(q * PART, PART)]
        return remote(view, view, self.ssem.at[kind, n], self.rsem.at[kind, n], self.i, target)

    def own(self, n):
        self.copy(0, n, self.h, self.xp).start()
        self.copy(1, n, self.h, self.up).start()
        self.copy(2, n, self.h, self.down).start()

    def pass_on(self, n):
        self.copy(0, n, self.xp, self.xp).wait_recv()
        self.copy(3, n, self.xp, self.up).start()
        self.copy(4, n, self.xp, self.down).start()
        if n % 2 == 0:
            self.copy(1, n, self.down, self.up).wait_recv()
            self.copy(5, n, self.down, self.up).start()
        else:
            self.copy(2, n, self.up, self.down).wait_recv()
            self.copy(5, n, self.up, self.down).start()

    def far_on(self, n):
        self.copy(5, n, self.far, self.up).wait_recv()
        self.copy(6, n, self.far, self.xp).start()

    def whole(self, n):
        if n % 2 == 0:
            self.copy(2, n, self.up, self.up).wait_recv()
        else:
            self.copy(1, n, self.down, self.up).wait_recv()
        self.copy(3, n, self.pdown, self.up).wait_recv()
        self.copy(4, n, self.pup, self.up).wait_recv()
        self.copy(6, n, self.pfar, self.up).wait_recv()

    def drain(self):
        for n in range(len(self.parts)):
            self.copy(0, n, self.h, self.xp).wait_send()
            self.copy(1, n, self.h, self.up).wait_send()
            self.copy(2, n, self.h, self.down).wait_send()
            self.copy(3, n, self.xp, self.up).wait_send()
            self.copy(4, n, self.xp, self.down).wait_send()
            self.copy(5, n, self.down, self.up).wait_send()
            self.copy(6, n, self.far, self.xp).wait_send()


def key_flow(kv, zs, zr, ks, kr):
    i, h = coords()
    xh, z, core = i // 16, lax.rem(i // 2, 8), lax.rem(i, 2)
    up, down = ctx_of(xh, z + 1, core), ctx_of(xh, z - 1, core)
    twin = ctx_of(xh, z, 1 - core)
    lanes = [(k, d) for k in range(2) for d in range(2)]

    def hops(k, d):
        return 4 if k == d else 3

    def view(k, dz, c):
        return kv.at[lax.rem(z + dz + 8, 8) * 2 + c, k]

    def ring(k, d, s):
        v = view(k, -s if d == 0 else s, core)
        return remote(v, v, zs.at[k, d, s], zr.at[k, d, s], up if d == 0 else down, h)

    def landed(k, d, s):
        v = view(k, -s - 1 if d == 0 else s + 1, core)
        return remote(v, v, zs.at[k, d, s], zr.at[k, d, s], up if d == 0 else down, h)

    def share(k, dz, c):
        v = view(k, dz, c)
        return remote(v, v, ks.at[k, dz % 8], kr.at[k, dz % 8], twin, h)

    for k, d in lanes:
        ring(k, d, 0).start()
    for k in range(2):
        share(k, 0, core).start()
    yield
    for s in range(4):
        for k, d in lanes:
            if s < hops(k, d):
                landed(k, d, s).wait_recv()
                if s + 1 < hops(k, d):
                    ring(k, d, s + 1).start()
                share(k, -s - 1 if d == 0 else s + 1, core).start()
        yield
    for k in range(2):
        for dz in range(-4, 4):
            share(k, dz, 1 - core).wait_recv()
    yield
    for k, d in lanes:
        for s in range(hops(k, d)):
            ring(k, d, s).wait_send()
    for k in range(2):
        for dz in range(-4, 4):
            share(k, dz, core).wait_send()
    yield


def to_rows(columns):
    lane = lax.broadcasted_iota(jnp.int32, (TOK, TOK), 1)
    packed = jnp.zeros((TOK, TOK), F32)
    for k, c in enumerate(columns):
        packed = jnp.where(lane == k, c, packed)
    return packed.T[0:8]


def to_columns(rows):
    return jnp.concatenate([rows, jnp.zeros((TOK - 8, TOK), F32)], axis=0).T


def layer_kernel(q_in, k_in, v_in, w_in, res_in, gain, ids_in, cw_in, wg_in, wu_in, wd_in, cot_in,
                 moe_out, attg_out, resg_out, gaing_out, combg_out, dgate_out, dup_out, ddown_out,
                 qb, kv, w_ref, res, ids_ref, cw_ref, wg, wu, wd, cot_ref,
                 place, whi, wlo, packed, gcot, gin, ob, os, terms, got, stats, stats2, normed, inv,
                 act_s, gd_s, ud_s, gp_s, up_s, t_ref, r_ref, fin, picked, rgb, gsum,
                 moe, attg, resg, gaing, combg, dgate, dup, ddown,
                 lsem, osem, zs, zr, ks, kr, xs, xr, asend, arecv, gs, gr, ts, tr, ss, sr,
                 fs, fr, bs, br, rs, rr, qs, qr):
    i, h = coords()
    xh, z, core = i // 16, lax.rem(i // 2, 8), lax.rem(i, 2)
    xl, y = h // 4, lax.rem(h, 4)
    xp, up, down = head_of(1 - xl, y), head_of(xl, y + 1), head_of(xl, y - 1)
    pup, pdown = head_of(1 - xl, y + 1), head_of(1 - xl, y - 1)
    far, pfar = head_of(xl, y + 2), head_of(1 - xl, y + 2)
    other = ctx_of(1 - xh, z, core)
    HR = ROWS // 2
    seat = lax.rem(i, 16)

    loads = [
        pltpu.make_async_copy(s, d, lsem.at[n])
        for n, (s, d) in enumerate((
            (k_in, kv.at[seat, 0]), (v_in, kv.at[seat, 1]), (q_in, qb.at[0]), (ids_in, ids_ref), (cw_in, cw_ref),
            (cot_in, cot_ref), (w_in, w_ref), (res_in, res), (wg_in, wg), (wu_in, wu), (wd_in, wd),
        ))
    ]
    for c in loads:
        c.start()
    bar = pltpu.get_barrier_semaphore()
    greet(bar)
    for c in loads[3:6]:
        c.wait()
    pad = jnp.zeros((TOK - TOP, TOK), F32)
    ids = jnp.concatenate([ids_ref[...].astype(F32), pad], axis=0).T.astype(jnp.int32)
    cw = jnp.concatenate([cw_ref[...], pad], axis=0).T
    p, hi, lo = routing(ids, cw)
    place[...] = p
    whi[...] = hi
    wlo[...] = lo
    cot = cot_ref[...]
    rows = dot(hi, cot, 0, 0) + dot(lo, cot, 0, 0)
    packed[0] = rows.astype(BF).reshape(2, ROWS, W)
    for c in loads[0:3]:
        c.wait()
    pl.semaphore_wait(bar, NC - 1 + NH - 1)

    def sent(part, g, e):
        return dispatched(packed.at[part], g, asend.at[part], arecv.at[part], e)

    keys = key_flow(kv, zs, zr, ks, kr)
    next(keys)
    q_swap = remote(qb.at[0], qb.at[1], xs.at[0], xr.at[0], other, h)
    q_swap.start()
    cots = HeadGather(gcot, gs.at[0], gr.at[0])
    next(keys)
    next(keys)
    next(keys)
    start_dispatch(packed.at[0], gcot, asend.at[0], arecv.at[0], lsem.at[11], 0)
    next(keys)
    start_dispatch(packed.at[0], gcot, asend.at[0], arecv.at[0], lsem.at[11], 1)
    next(keys)

    q_swap.wait_recv()
    q2 = jnp.concatenate([qb[0], qb[1]], axis=0)
    r = lax.broadcasted_iota(jnp.int32, (2 * TOK, 1), 0)
    limit = jnp.where(r < TOK, seat * TOK + r, jnp.where(xh == 0, 16 * TOK - 1, -1))
    allowed = lax.broadcasted_iota(jnp.int32, (2 * TOK, 16 * TOK), 1) <= limit
    outs, tops, sums = [], [], []
    for n in range(2):
        cs = slice(n * DH, (n + 1) * DH)
        s = dot(q2[:, cs], kv[:, 0, :, cs].reshape(16 * TOK, DH), 1, 1) * DH ** (-0.5)
        s = jnp.where(allowed, s, -1e30)
        m = jnp.max(s, axis=1, keepdims=True)
        wts = jnp.exp(s - m)
        tot = jnp.sum(wts, axis=1, keepdims=True)
        o = dot(wts.astype(BF), kv[:, 1, :, cs].reshape(16 * TOK, DH)) / tot
        outs.append(o)
        tops.append(m)
        sums.append(tot)
    seen = jnp.where(xh == 0, 1.0, 0.0)
    ob[0] = jnp.concatenate([o[TOK:] for o in outs], axis=1).astype(BF)
    os[0] = to_rows([tops[0][TOK:], sums[0][TOK:] * seen, tops[1][TOK:], sums[1][TOK:] * seen])
    o_swap = remote(ob.at[0], ob.at[1], xs.at[1], xr.at[1], other, h)
    s_swap = remote(os.at[0], os.at[1], xs.at[2], xr.at[2], other, h)
    o_swap.start()
    s_swap.start()
    sent(0, gcot, 0).wait_recv()
    cots.own(0)
    cots.own(1)
    loads[6].wait()
    loads[7].wait()
    s_swap.wait_recv()
    o_swap.wait_recv()
    there = to_columns(os[1])
    att = []
    for n in range(2):
        m1, l1 = tops[n][:TOK], sums[n][:TOK]
        m2, l2 = there[:, 2 * n : 2 * n + 1], there[:, 2 * n + 1 : 2 * n + 2]
        m = jnp.maximum(m1, m2)
        a1, a2 = l1 * jnp.exp(m1 - m), l2 * jnp.exp(m2 - m)
        o2 = ob[1, :, n * DH : (n + 1) * DH].astype(F32)
        att.append((a1 * outs[n][:TOK] + a2 * o2) / (a1 + a2))
    att = jnp.concatenate(att, axis=1).astype(BF)

    t = dot(att, w_ref[...]).astype(BF)
    for d in range(NH):
        terms[d] = t[:, d * W : (d + 1) * W]
    for o in range(1, NH):
        d = lax.rem(h + o, NH)
        remote(terms.at[d], got.at[o], ts.at[o], tr.at[o], i, d).start()

    cots.pass_on(0)
    hidden = res[...].astype(F32) + terms[h].astype(F32)
    for o in range(1, NH):
        d = lax.rem(h + o, NH)
        remote(terms.at[d], got.at[o], ts.at[o], tr.at[o], i, d).wait()
        hidden = hidden + got[o].astype(F32)
    stats[0] = to_rows([jnp.sum(hidden * hidden, axis=1, keepdims=True)])
    for o in range(1, NH):
        remote(stats.at[0], stats.at[o], ss.at[0, o], sr.at[0, o], i, lax.rem(h + o, NH)).start()
    sent(0, gcot, 1).wait_recv()
    cots.own(2)
    cots.own(3)
    cots.pass_on(1)
    cots.far_on(0)
    total = stats[0]
    for o in range(1, NH):
        remote(stats.at[0], stats.at[o], ss.at[0, o], sr.at[0, o], i, lax.rem(h + o, NH)).wait()
        total = total + stats[o]
    inverse = lax.rsqrt(to_columns(total)[:, 0:1] / D + 1e-06)
    inv[...] = jnp.broadcast_to(inverse, (TOK, TOK))
    nrm = hidden * inverse
    normed[...] = nrm
    inputs = (nrm * gain[...]).astype(BF)
    packed[1] = dot(place[...], inputs, 0, 0).astype(BF).reshape(2, ROWS, W)
    start_dispatch(packed.at[1], gin, asend.at[1], arecv.at[1], lsem.at[11], 0)
    start_dispatch(packed.at[1], gin, asend.at[1], arecv.at[1], lsem.at[11], 1)
    cots.pass_on(2)
    cots.far_on(1)
    cots.pass_on(3)
    for c in loads[8:]:
        c.wait()

    def rows_of(ref, e, lo, n):
        return jnp.concatenate([ref[b, e, lo : lo + n] for b in range(NH)], axis=1)

    def forward(e, hf):
        sl = slice(hf * HR, (hf + 1) * HR)
        x = rows_of(gin, e, hf * HR, HR)
        gp = dot(x, wg[e], 1, 1)
        u = dot(x, wu[e], 1, 1)
        gp_s[e, sl] = gp
        up_s[e, sl] = u
        act = (gp * jax.nn.sigmoid(gp) * u).astype(BF)
        act_s[e, sl] = act
        for b in range(NH):
            t_ref[0, b, e, sl] = dot(act, wd[e, :, b * W : (b + 1) * W]).astype(BF)

    def backward(e, hf):
        sl = slice(hf * HR, (hf + 1) * HR)
        x = rows_of(gcot, e, hf * HR, HR)
        ag = dot(x, wd[e], 1, 1)
        gp = gp_s[e, sl]
        s = jax.nn.sigmoid(gp)
        gd = (ag * up_s[e, sl] * s * (1.0 + gp * (1.0 - s))).astype(BF)
        ud = (ag * gp * s).astype(BF)
        gd_s[e, sl] = gd
        ud_s[e, sl] = ud
        for b in range(NH):
            cs = slice(b * W, (b + 1) * W)
            t_ref[1, b, e, sl] = (dot(gd, wg[e, :, cs]) + dot(ud, wu[e, :, cs])).astype(BF)

    def weight_grads(e):
        for b in range(NH):
            cs = slice(b * W, (b + 1) * W)
            x = gin[b, e]
            dgate[e, :, cs] = dot(gd_s[e], x, 0, 0).astype(BF)
            dup[e, :, cs] = dot(ud_s[e], x, 0, 0).astype(BF)
            ddown[e, :, cs] = dot(act_s[e], gcot[b, e], 0, 0).astype(BF)

    def tview(f, block):
        t, e, q = f
        return t_ref.at[t, block, e, pl.ds(q * PART, PART)]

    def index(f):
        return (f[0] * 2 + f[1]) * PARTS + f[2]

    def copy(kind, f, block, target):
        n = index(f)
        return remote(tview(f, block), r_ref.at[n, kind], fs.at[kind, n], fr.at[kind, n], i, target)

    def add(f, block, kinds):
        acc = tview(f, block)[...].astype(F32)
        for kind in kinds:
            acc = acc + r_ref[index(f), kind].astype(F32)
        return acc.astype(BF)

    def stage0(f):
        copy(0, f, pfar, xp).start()
        copy(1, f, pup, up).start()
        copy(2, f, pdown, down).start()
        if f[2] % 2 == 0:
            copy(6, f, down, down).start()
        else:
            copy(5, f, up, up).start()

    def stage1(f):
        copy(0, f, far, xp).wait_recv()
        tview(f, far)[...] = add(f, far, (0,))
        copy(3, f, far, up if f[2] % 2 == 0 else down).start()
        copy(1, f, xp, up).wait_recv()
        copy(2, f, xp, up).wait_recv()
        tview(f, xp)[...] = add(f, xp, (1, 2))
        copy(4, f, xp, xp).start()

    def stage2(f):
        block = up if f[2] % 2 == 0 else down
        copy(3, f, block, up).wait_recv()
        tview(f, block)[...] = add(f, block, (3,))
        copy(5 if f[2] % 2 == 0 else 6, f, block, block).start()

    def stage3(f):
        t, e, q = f
        for kind in (4, 5, 6):
            copy(kind, f, h, up).wait_recv()
        fin[t, e, q * PART : (q + 1) * PART] = add(f, h, (4, 5, 6))

        def send(k, c):
            d = q * (PART // CAP) + k

            @pl.when(d != i)
            def _():
                back(t, e, d).start()

            return c

        lax.fori_loop(0, PART // CAP, send, 0)

    def back(t, e, d):
        return remote(fin.at[t, e, pl.ds(pl.multiple_of(d * CAP, CAP), CAP)], picked.at[t, e, i],
                      bs.at[t, e], br.at[t, e], d, h)

    def drain(f):
        for kind, block in ((0, pfar), (1, pup), (2, pdown), (3, far), (4, xp), (5, up), (6, down)):
            copy(kind, f, block, xp).wait_send()

    flows = [(t, e, q) for t in range(2) for e in range(2) for q in range(PARTS)]
    count = len(flows)
    outward = [
        pltpu.make_async_copy(s, d, osem.at[n])
        for n, (s, d) in enumerate((
            (moe, moe_out), (attg, attg_out), (resg, resg_out), (gaing, gaing_out), (combg, combg_out),
            (dgate, dgate_out), (dup, dup_out), (ddown, ddown_out),
        ))
    ]

    def landed(t):
        mine = pl.ds(pl.multiple_of(i * CAP, CAP), CAP)
        for e in range(2):
            own = pltpu.make_async_copy(fin.at[t, e, mine], picked.at[t, e, i], lsem.at[11])
            own.start()
            own.wait()
            part = picked.at[t, e, pl.ds(0, NC - 1)]
            remote(part, part, bs.at[t, e], br.at[t, e], i, xp).wait()
        return picked[t].reshape(SLOTS, W)

    def combine():
        rows = landed(0)
        moe[...] = (dot(whi[...], rows) + dot(wlo[...], rows)).astype(BF)
        outward[0].start()
        every = dot(cot_ref[...], rows, 1, 1) * place[...].astype(F32)
        n = lax.broadcasted_iota(jnp.int32, (TOK, SLOTS), 1)
        expert = 2 * (lax.rem(n, ROWS) // CAP) + n // ROWS
        columns = [
            jnp.sum(jnp.where(expert == ids[:, k : k + 1], every, 0.0), axis=1, keepdims=True) for k in range(TOP)
        ]
        return columns

    def tick(n):
        if n < count:
            t, e, q = flows[n]
            (forward if t == 0 else backward)(e, q)
            stage0(flows[n])
        if 0 <= n - 1 < count:
            stage1(flows[n - 1])
        if 0 <= n - 2 < count:
            stage2(flows[n - 2])
        if 0 <= n - 3 < count:
            stage3(flows[n - 3])

    ins = HeadGather(gin, gs.at[1], gr.at[1])
    sent(1, gin, 0).wait_recv()
    ins.own(0)
    cots.far_on(2)
    ins.own(1)
    cots.far_on(3)
    ins.pass_on(0)
    sent(1, gin, 1).wait_recv()
    ins.own(2)
    ins.pass_on(1)
    ins.far_on(0)
    ins.own(3)
    ins.pass_on(2)
    ins.far_on(1)
    ins.whole(0)
    tick(0)
    ins.pass_on(3)
    ins.far_on(2)
    ins.whole(1)
    tick(1)
    ins.far_on(3)
    ins.whole(2)
    tick(2)
    ins.whole(3)
    tick(3)
    for n in range(4):
        cots.whole(n)
    for n in range(2 * PARTS, count + 3):
        tick(n)

    columns = combine()
    rows = landed(1)
    input_grad = dot(place[...], rows)
    nrm = normed[...]
    gsum[0] = jnp.broadcast_to(jnp.sum(input_grad * nrm, axis=0, keepdims=True), (8, W))

    def gain_copy(o):
        d = lax.rem(i + o, NC)
        return remote(gsum.at[0], gsum.at[o], qs.at[o], qr.at[o], d, h)

    def gain_start(o, c):
        gain_copy(o).start()
        return c

    ng = input_grad * gain[...]
    stats2[0] = to_rows(columns + [jnp.sum(ng * nrm, axis=1, keepdims=True)])
    for o in range(1, NH):
        remote(stats2.at[0], stats2.at[o], ss.at[1, o], sr.at[1, o], i, lax.rem(h + o, NH)).start()
    lax.fori_loop(1, NC, gain_start, 0)
    total = stats2[0]
    for o in range(1, NH):
        remote(stats2.at[0], stats2.at[o], ss.at[1, o], sr.at[1, o], i, lax.rem(h + o, NH)).wait()
        total = total + stats2[o]
    combg[...] = total[0:TOP]
    outward[4].start()
    centre = to_columns(total)[:, TOP : TOP + 1] / D
    rg = (inv[:, 0:1] * (ng - nrm * centre)).astype(BF)
    resg[...] = rg
    outward[2].start()
    rgb[h] = rg
    for o in range(1, NH):
        d = lax.rem(h + o, NH)
        remote(rgb.at[h], rgb.at[h], rs.at[o], rr.at[o], i, d).start()

    weight_grads(0)
    weight_grads(1)
    for c in outward[5:]:
        c.start()

    def gain_wait(o, c):
        gain_copy(o).wait()
        return c + gsum[o]

    gaing[...] = lax.fori_loop(1, NC, gain_wait, gsum[0])[0:1]
    outward[3].start()
    for f in flows:
        drain(f)
    for part in range(2):
        for e in range(2):
            sent(part, (gcot, gin)[part], e).wait_send()
    cots.drain()
    ins.drain()
    q_swap.wait_send()
    o_swap.wait_send()
    s_swap.wait_send()
    for _ in keys:
        pass
    for o in range(1, NH):
        s = lax.rem(h - o + NH, NH)
        remote(rgb.at[s], rgb.at[s], rs.at[o], rr.at[o], i, s).wait()
    whole = jnp.concatenate([rgb[b] for b in range(NH)], axis=1)
    attg[...] = dot(whole, w_ref[...], 1, 1).astype(BF)
    outward[1].start()
    for c in outward:
        c.wait()


VM = pl.BlockSpec(memory_space=pltpu.VMEM)
ANY = pl.BlockSpec(memory_space=pl.ANY)
DMA = pltpu.SemaphoreType.DMA
SDS = jax.ShapeDtypeStruct
RESULTS = (
    ((TOK, W), BF), ((TOK, W), BF), ((TOK, W), BF), ((1, W), F32), ((TOP, TOK), F32),
    ((2, FD, D), BF), ((2, FD, D), BF), ((2, FD, D), BF),
)


def call_layer(*args):
    v = pltpu.VMEM
    return pl.pallas_call(
        layer_kernel,
        out_shape=tuple(SDS(s, t) for s, t in RESULTS),
        in_specs=[ANY] * 5 + [VM] + [ANY] * 6,
        out_specs=(ANY,) * 8,
        scratch_shapes=[
            v((2, TOK, W), BF), v((16, 2, TOK, W), BF), v((W, D), BF), v((TOK, W), BF),
            v((TOP, TOK), jnp.int32), v((TOP, TOK), F32),
            v((2, FD, D), BF), v((2, FD, D), BF), v((2, FD, D), BF), v((TOK, W), BF),
            v((TOK, SLOTS), BF), v((TOK, SLOTS), BF), v((TOK, SLOTS), BF),
            v((2, 2, ROWS, W), BF), v((NH, 2, ROWS, W), BF), v((NH, 2, ROWS, W), BF),
            v((2, TOK, W), BF), v((2, 8, TOK), F32), v((NH, TOK, W), BF), v((NH, TOK, W), BF),
            v((NH, 8, TOK), F32), v((NH, 8, TOK), F32), v((TOK, W), F32), v((TOK, TOK), F32),
            v((2, ROWS, FD), BF), v((2, ROWS, FD), BF), v((2, ROWS, FD), BF),
            v((2, ROWS, FD), F32), v((2, ROWS, FD), F32),
            v((2, NH, 2, ROWS, W), BF), v((4 * PARTS, 7, PART, W), BF), v((2, 2, ROWS, W), BF),
            v((2, 2, NC, CAP, W), BF), v((NH, TOK, W), BF), v((NC, 8, W), F32),
            *[v(s, t) for s, t in RESULTS],
            DMA((12,)), DMA((8,)),
            DMA((2, 2, 4)), DMA((2, 2, 4)), DMA((2, 8)), DMA((2, 8)), DMA((3,)), DMA((3,)),
            DMA((2, 2)), DMA((2, 2)), DMA((2, 7, 2 * PARTS)), DMA((2, 7, 2 * PARTS)), DMA((NH,)), DMA((NH,)),
            DMA((2, NH)), DMA((2, NH)),
            DMA((7, 4 * PARTS)), DMA((7, 4 * PARTS)), DMA((2, 2)), DMA((2, 2)), DMA((NH,)), DMA((NH,)), DMA((NC,)), DMA((NC,)),
        ],
        compiler_params=pltpu.CompilerParams(collective_id=1, has_side_effects=True, vmem_limit_bytes=60 << 20),
        name="layer",
    )(*args)


def hand_on(*args):
    parts = [(n, None) for n in range(5)] + [(n, e) for n in range(5, 8) for e in range(2)]

    def kernel(*refs):
        into, sems = refs[16:24], refs[24]

        def at(ref, e):
            return ref if e is None else ref.at[e]

        ins = [pltpu.make_async_copy(at(refs[n], e), at(into[n], e), sems.at[0, k]) for k, (n, e) in enumerate(parts)]
        outs = [pltpu.make_async_copy(at(into[n], e), at(refs[n + 8], e), sems.at[1, k]) for k, (n, e) in enumerate(parts)]
        for c in ins:
            c.start()
        for a, b in zip(ins, outs):
            a.wait()
            b.start()
        for c in outs:
            c.wait()

    return pl.pallas_call(
        kernel,
        out_shape=tuple(SDS(s, t) for s, t in RESULTS),
        in_specs=[ANY] * 8,
        out_specs=(ANY,) * 8,
        scratch_shapes=[pltpu.VMEM(s, t) for s, t in RESULTS] + [DMA((2, 11))],
        compiler_params=pltpu.CompilerParams(vmem_limit_bytes=60 << 20),
        name="hand_on",
    )(*args)


def per_device(queries, key_rows, value_rows, output_weight, residual_stream, norm_gain, expert_ids,
               combine_weights, gate_weight, up_weight, down_weight, cotangent):
    results = call_layer(
        queries, key_rows, value_rows, output_weight, residual_stream, norm_gain.reshape(1, W), expert_ids.T,
        combine_weights.T, gate_weight, up_weight, down_weight, cotangent)
    moe, attg, resg, gaing, combg, dgate, dup, ddown = hand_on(*results)
    return moe, attg, resg, gaing.reshape(W), combg.T, dgate, dup, ddown


def solution(mesh):
    return jax.shard_map(
        per_device,
        mesh=mesh,
        in_specs=(
            P("ctx", "head"), P("ctx", "head"), P("ctx", "head"), P("head", None), P("ctx", "head"), P("head"),
            P("ctx", None), P("ctx", None), P("ctx", "head", None), P("ctx", "head", None),
            P("ctx", "head", None), P("ctx", "head"),
        ),
        out_specs=(
            P("ctx", "head"), P("ctx", "head"), P("ctx", "head"), P("head"), P("ctx", None),
            P("ctx", "head", None), P("ctx", "head", None), P("ctx", "head", None),
        ),
        check_vma=False,
    )
```
